256 devices in a mesh: space: 16 (over y, z_lo), mode: 16 (over x, z_hi, core).
Axes of the slice: x: 4, y: 4, z: 8 (z_hi: 2, z_lo: 4; z = z_hi * 4 + z_lo), core: 2. Of those that a mesh axis runs over, the one named last changes fastest.
Arguments:
- fields: bfloat16 [64, 8192, 512], P('mode', 'space'), may hold values from -6 to 6
- pre_act: bfloat16 [64, 8192, 512], P('mode', 'space'), may hold values from -6 to 6
- cotangent: bfloat16 [64, 8192, 512], P('mode', 'space'), may hold values from -3 to 3
- weights: bfloat16 [64, 2, 512, 512], P('mode'), may hold values from -0.1875 to 0.1875
Outputs:
- field_grad: bfloat16 [64, 8192, 512], P('mode', 'space')
- weight_grad: float32 [64, 2, 512, 512], P('mode', None, None, 'space')
The draws below stay inside these ranges and needn't reach their ends.
All inputs are finite; a program needn't handle non-finite values.
Results may differ from the reference program's by a relative error of at most 0.0072.
Values may be sent and summed in bfloat16 or wider, within the bound.
No kernel may reach another device: no remote copies, remote signals or barrier semaphores. Data moves between devices by JAX's collectives and lax.ppermute only.
A program may use at most 64 MiB of HBM per device.

```python
import math
import jax
import jax.numpy as jnp
from jax import lax

C = 512
MODES = 64
B = 64
X = 8192


def block_scale(rng, dims, cuts, smallest, largest):
    loudness = 1.0
    for dim, shards_of in cuts:
        heights = jax.random.uniform(jax.random.fold_in(jax.random.fold_in(rng, 6), dim), (shards_of,), jnp.float32, smallest / len(cuts), largest / len(cuts))
        loudness = loudness * jnp.repeat(jnp.exp(heights), dims[dim] // shards_of).reshape((-1,) + (1,) * (len(dims) - 1 - dim))
    return loudness


def gaussian(key, shape, spread, bound, shards=(), held_as=jnp.bfloat16):
    values = spread * jax.random.normal(key, shape, jnp.float32)
    if shards:
        values = values * block_scale(key, shape, shards, -0.22, 0.18)
    return jnp.clip(values, -bound, bound).astype(held_as)


def setup_inputs(seed: int = 0) -> dict:
    arg_keys = jax.random.split(jax.random.key(seed), 5)
    return {
        "fields": gaussian(arg_keys[0], (B, X, C), 1.0, 6.0, ((0, 16), (1, 16))),
        "pre_act": gaussian(arg_keys[1], (B, X, C), 1.0, 6.0, ((0, 16), (1, 16))),
        "cotangent": gaussian(arg_keys[2], (B, X, C), 0.5, 3.0, ((0, 16), (1, 16))),
        "weights": gaussian(arg_keys[3], (MODES, 2, C, C), (2 * C) ** -0.5, 0.1875, ((0, 16),)),
    }


def make_table(n_modes, points, offset, total):
    wave_nums = jnp.arange(n_modes, dtype=jnp.int32)
    position = jnp.arange(points, dtype=jnp.int32) + offset
    phases = wave_nums[:, None] * position[None, :] % total
    angles = phases.astype(jnp.float32) * (2.0 * math.pi / total)
    return jnp.stack([jnp.cos(angles), -jnp.sin(angles)], axis=1).astype(jnp.bfloat16)

def gelu_slope(values):
    normal_cdf = 0.5 * (1.0 + jax.scipy.special.erf(values / math.sqrt(2.0)))
    density = jnp.exp(-0.5 * values * values) / math.sqrt(2.0 * math.pi)
    return normal_cdf + values * density

def lowered(values):
    return lax.optimization_barrier(values.astype(jnp.bfloat16)).astype(jnp.float32)

def reference(fields, pre_act, cotangent, weights):
    factor = float(X) ** (-0.5)
    table = make_table(MODES, X, 0, X).astype(jnp.float32)
    spec_u = jnp.einsum('kpx,bxc->kpbc', table, fields.astype(jnp.float32)) * factor
    slopes = (cotangent.astype(jnp.float32) * gelu_slope(pre_act.astype(jnp.float32))).astype(jnp.bfloat16)
    weight_k = jnp.where(jnp.arange(MODES) == 0, 1.0, 2.0).astype(jnp.float32) * factor
    spec_g = jnp.einsum('kpx,bxc->kpbc', table, slopes.astype(jnp.float32)) * weight_k[:, None, None, None]
    input_low = lowered(spec_u)
    grad_low = lowered(spec_g)
    u_real, u_imag = (input_low[:, 0], input_low[:, 1])
    g_real, g_imag = (grad_low[:, 0], grad_low[:, 1])
    grad_real = jnp.einsum('mbc,mbd->mcd', u_real, g_real) + jnp.einsum('mbc,mbd->mcd', u_imag, g_imag)
    grad_imag = jnp.einsum('mbc,mbd->mcd', u_real, g_imag) - jnp.einsum('mbc,mbd->mcd', u_imag, g_real)
    weight_grad = jnp.stack([grad_real, grad_imag], axis=1)
    w_real = weights[:, 0].astype(jnp.float32)
    w_imag = weights[:, 1].astype(jnp.float32)
    mode_real = jnp.einsum('mbd,mcd->mbc', g_real, w_real) + jnp.einsum('mbd,mcd->mbc', g_imag, w_imag)
    mode_imag = jnp.einsum('mbd,mcd->mbc', g_imag, w_real) - jnp.einsum('mbd,mcd->mbc', g_real, w_imag)
    mode_grad = lowered(jnp.stack([mode_real, mode_imag], axis=1))
    field_grad = (jnp.einsum('kpbc,kpx->bxc', mode_grad, table) * factor).astype(jnp.bfloat16)
    return (field_grad, weight_grad)
```

```python
import functools
import math

import jax
import jax.numpy as jnp
from jax import lax
from jax.experimental import pallas as pl
from jax.experimental.pallas import tpu as pltpu
from jax.sharding import Mesh
from jax.sharding import PartitionSpec as P

F32, BF16 = jnp.float32, jnp.bfloat16
FIRST = ("y", "x")
SECOND = ("zl", "w")
NT = (((1,), (1,)), ((), ()))
TN = (((0,), (0,)), ((), ()))


def make_table(n_modes, points, offset, total):
    wave_nums = jnp.arange(n_modes, dtype=jnp.int32)
    position = jnp.arange(points, dtype=jnp.int32) + offset
    phases = wave_nums[:, None] * position[None, :] % total
    angles = phases.astype(F32) * (2.0 * math.pi / total)
    return jnp.concatenate([jnp.cos(angles), -jnp.sin(angles)], axis=0).astype(BF16)


def gelu_slope(values):
    normal_cdf = 0.5 * (1.0 + lax.erf(values * (1.0 / math.sqrt(2.0))))
    density = jnp.exp(-0.5 * values * values) * (1.0 / math.sqrt(2.0 * math.pi))
    return normal_cdf + values * density


def dot(a, b, dims=None):
    if dims is None:
        return jnp.dot(a, b, preferred_element_type=F32)
    return lax.dot_general(a, b, dims, preferred_element_type=F32)


def row_moves(n, digits):
    row = lax.broadcasted_iota(jnp.int32, (n, n), 0)
    col = lax.broadcasted_iota(jnp.int32, (n, n), 1)
    source = jnp.zeros((n, n), jnp.int32)
    for out_stride, size, in_stride in digits:
        digit = (row >> (out_stride.bit_length() - 1)) & (size - 1)
        source = source + (digit << (in_stride.bit_length() - 1))
    return jnp.where(source == col, 1.0, 0.0).astype(BF16)


def turned(n):
    row = lax.broadcasted_iota(jnp.int32, (n, n), 0)
    col = lax.broadcasted_iota(jnp.int32, (n, n), 1)
    sign = jnp.where((row & 4) == 0, 1.0, -1.0)
    return jnp.where((row ^ 4) == col, sign, 0.0).astype(BF16)


def gather_lanes(values, quarter):
    lane = lax.broadcasted_iota(jnp.int32, (values.shape[0], 128), 1) >> 5
    out = None
    for j in range(4):
        block = values[:, 128 * j : 128 * j + 128]
        shift = (32 * (j - quarter)) % 128
        if shift:
            block = pltpu.roll(block, shift, 1)
        out = block if out is None else jnp.where(lane == j, block, out)
    return out


def spectra_kernel(table_ref, fields_ref, pre_ref, cot_ref, out_ref, table_u):
    @pl.when((pl.program_id(0) == 0) & (pl.program_id(1) == 0))
    def _():
        moves = row_moves(128, [(64, 2, 64), (16, 4, 1), (4, 4, 16), (1, 4, 4)])
        table_u[...] = dot(moves, table_ref[...]).astype(BF16)

    spec_u = dot(table_u[...], fields_ref[0]).astype(BF16)
    slopes = cot_ref[0].astype(F32) * gelu_slope(pre_ref[0].astype(F32))
    spec_g = dot(table_ref[...], slopes.astype(BF16)).astype(BF16)
    for j in range(4):
        for p in range(2):
            rows = slice(64 * p + 16 * j, 64 * p + 16 * j + 16)
            out_ref[j, 16 * p : 16 * p + 16, :] = spec_g[rows]
            out_ref[j, 32 + 16 * p : 48 + 16 * p, :] = spec_u[rows]


def sum_y_kernel(in_ref, out_ref):
    total = in_ref[0:4].astype(F32)
    for y in range(1, 4):
        total = total + in_ref[4 * y : 4 * y + 4].astype(F32)
    low = total.astype(BF16)
    g = low[:, :32].reshape(128, 512)
    u = low[:, 32:].reshape(128, 512)
    g = dot(row_moves(128, [(32, 4, 1), (8, 4, 4), (4, 2, 16), (1, 4, 32)]), g)
    u = dot(row_moves(128, [(32, 4, 32), (8, 4, 4), (4, 2, 16), (1, 4, 1)]), u)
    for i in range(16):
        both = jnp.concatenate([g[8 * i : 8 * i + 8], u[8 * i : 8 * i + 8]], axis=0)
        out_ref[i] = both.astype(BF16)


def modes_kernel(factor, where_ref, in_ref, w_ref, out_ref):
    total = in_ref[0:4].astype(F32)
    for zl in range(1, 4):
        total = total + in_ref[4 * zl : 4 * zl + 4].astype(F32)
    first_mode = (where_ref[0] == 0) & (where_ref[1] == 0) & (where_ref[2] == 0)
    g = total[:, :8].reshape(32, 512) * jnp.where(first_mode, factor, 2.0 * factor)
    u = total[:, 8:].reshape(32, 512) * factor
    g_low = g.astype(BF16)
    u = dot(row_moves(32, [(8, 4, 1), (4, 2, 4), (1, 4, 8)]), u.astype(BF16))
    g_turned = dot(turned(32), g_low).astype(BF16)
    grad = dot(g_low, w_ref[0], NT) + dot(g_turned, w_ref[1], NT)
    for zl in range(4):
        lanes = gather_lanes(g, zl)
        chunk = jnp.concatenate([lanes[8 * w : 8 * w + 8] for w in range(4)], axis=1)
        for w in range(4):
            rows = slice(8 * w, 8 * w + 8)
            out_ref[4 * zl + w] = jnp.concatenate([grad[rows], u[rows], chunk], axis=0).astype(BF16)


def turn_kernel(where_ref, in_ref, out_ref):
    grad = in_ref[:, 0:8].astype(F32).reshape(128, 512).astype(BF16)
    u = in_ref[:, 8:16].astype(F32).reshape(128, 512).astype(BF16)
    grad = dot(row_moves(128, [(32, 4, 1), (16, 2, 4), (4, 4, 8), (1, 4, 32)]), grad)
    u = dot(row_moves(128, [(32, 4, 8), (8, 4, 1), (4, 2, 4), (1, 4, 32)]), u)
    mine = [in_ref[4 * ki + where_ref[1], 16:24, :].astype(F32) for ki in range(4)]
    for y in range(4):
        chunk = jnp.concatenate([gather_lanes(m, y) for m in mine], axis=1)
        for x in range(4):
            rows = slice(32 * x, 32 * x + 32)
            out_ref[4 * y + x] = jnp.concatenate([grad[rows], u[rows], chunk], axis=0).astype(BF16)


def last_kernel(factor, where_ref, in_ref, table_ref, field_ref, weight_ref):
    sub = pl.program_id(0)

    @pl.when(sub == 0)
    def _():
        g = jnp.concatenate(
            [in_ref[4 * s + where_ref[0], 64:72, :].astype(F32) for s in range(4)], axis=0
        )
        g_turned = dot(turned(32), g.astype(BF16))
        lane = lax.broadcasted_iota(jnp.int32, (32, 128), 1)
        for ki in range(4):
            one, two = (v[:, 128 * ki : 128 * ki + 128] for v in (g, g_turned))
            left, right = [], []
            for w in range(4):
                a = pltpu.roll(one, (128 - 32 * w) % 128, 1) if w else one
                b = pltpu.roll(two, (160 - 32 * w) % 128, 1) if w != 1 else two
                left.append(jnp.where(lane < 32, a, b))
                for s in range(4):
                    right.append(in_ref[4 * s + ki, 32 + 8 * w : 40 + 8 * w, :].astype(F32))
            left = jnp.concatenate(left, axis=0).astype(BF16)
            right = jnp.concatenate(right, axis=0).astype(BF16)
            grad = dot(left, right, TN)
            weight_ref[ki, 0] = grad[0:32]
            weight_ref[ki, 1] = grad[32:64]

    modes = jnp.concatenate(
        [in_ref[4 * sub + j, 16 * p : 16 * p + 16, :] for p in range(2) for j in range(4)], axis=0
    )
    field_ref[0] = (dot(table_ref[...], modes) * factor).astype(BF16)


def shards(fields, pre_act, cotangent, weights):
    points = fields.shape[1]
    total = points * lax.axis_size("y") * lax.axis_size("zl")
    factor = float(total) ** (-0.5)
    x, w, zl = lax.axis_index("x"), lax.axis_index("w"), lax.axis_index("zl")
    table = make_table(64, points, (lax.axis_index("y") * 4 + zl) * points, total)
    where = jnp.stack([x, w, zl]).astype(jnp.int32)
    smem = pl.BlockSpec(memory_space=pltpu.SMEM)
    vmem = pl.BlockSpec(memory_space=pltpu.VMEM)
    params = pltpu.CompilerParams(vmem_limit_bytes=40 * 2**20)

    half = pl.BlockSpec((1, 512, 256), lambda b, h: (b, 0, h))
    send = pl.pallas_call(
        spectra_kernel,
        grid=(4, 2),
        in_specs=[pl.BlockSpec((128, 512), lambda b, h: (0, 0)), half, half, half],
        out_specs=pl.BlockSpec((4, 64, 256), lambda b, h: (b, 0, h)),
        out_shape=jax.ShapeDtypeStruct((16, 64, 512), BF16),
        scratch_shapes=[pltpu.VMEM((128, 512), BF16)],
        compiler_params=params,
        name="spectra",
    )(table, fields, pre_act, cotangent)
    got = lax.all_to_all(send, FIRST, 0, 0, tiled=True)
    send = pl.pallas_call(
        sum_y_kernel,
        in_specs=[vmem],
        out_specs=vmem,
        out_shape=jax.ShapeDtypeStruct((16, 16, 512), BF16),
        compiler_params=params,
        name="sum_y",
    )(got)
    got = lax.all_to_all(send, SECOND, 0, 0, tiled=True)
    mine = lax.dynamic_index_in_dim(weights, zl, 0, keepdims=False)
    send = pl.pallas_call(
        functools.partial(modes_kernel, factor),
        in_specs=[smem, vmem, vmem],
        out_specs=vmem,
        out_shape=jax.ShapeDtypeStruct((16, 24, 512), BF16),
        compiler_params=params,
        name="modes",
    )(where, got, mine)
    got = lax.all_to_all(send, SECOND, 0, 0, tiled=True)
    send = pl.pallas_call(
        turn_kernel,
        in_specs=[smem, vmem],
        out_specs=vmem,
        out_shape=jax.ShapeDtypeStruct((16, 72, 512), BF16),
        compiler_params=params,
        name="turn",
    )(where, got)
    got = lax.all_to_all(send, FIRST, 0, 0, tiled=True)
    field_grad, weight_grad = pl.pallas_call(
        functools.partial(last_kernel, factor),
        grid=(4,),
        in_specs=[
            smem,
            pl.BlockSpec((16, 72, 512), lambda b: (0, 0, 0)),
            pl.BlockSpec((512, 128), lambda b: (0, 0)),
        ],
        out_specs=[
            pl.BlockSpec((1, 512, 512), lambda b: (b, 0, 0)),
            pl.BlockSpec((4, 2, 32, 512), lambda b: (0, 0, 0, 0)),
        ],
        out_shape=[
            jax.ShapeDtypeStruct((4, 512, 512), BF16),
            jax.ShapeDtypeStruct((4, 2, 32, 512), F32),
        ],
        compiler_params=params,
        name="last",
    )(where, got, table.T)
    return field_grad, jnp.swapaxes(weight_grad, 2, 3)


def solution(mesh):
    grid = Mesh(mesh.devices.reshape(4, 4, 4, 4), ("y", "zl", "x", "w"))
    space, mode = ("y", "zl"), ("x", "w")
    whole = P(mode, space, None)
    return jax.shard_map(
        shards,
        mesh=grid,
        in_specs=(whole, whole, whole, P(mode, None, None, None)),
        out_specs=(whole, P(mode, None, None, space)),
        check_vma=False,
    )
```

```python
import functools
import math

import jax
import jax.numpy as jnp
from jax import lax
from jax.experimental import pallas as pl
from jax.experimental.pallas import tpu as pltpu
from jax.sharding import Mesh
from jax.sharding import PartitionSpec as P

F32, BF16 = jnp.float32, jnp.bfloat16
FIRST = ("y", "x")
SECOND = ("zl", "w")
SPECTRA_VMEM = 61 * 2**20
NT = (((1,), (1,)), ((), ()))
TN = (((0,), (0,)), ((), ()))


def make_table(n_modes, points, offset, total):
    wave_nums = jnp.arange(n_modes, dtype=jnp.int32)
    position = jnp.arange(points, dtype=jnp.int32) + offset
    phases = wave_nums[:, None] * position[None, :] % total
    angles = phases.astype(F32) * (2.0 * math.pi / total)
    return jnp.concatenate([jnp.cos(angles), -jnp.sin(angles)], axis=0).astype(BF16)


def gelu_slope(values):
    normal_cdf = 0.5 * (1.0 + lax.erf(values * (1.0 / math.sqrt(2.0))))
    density = jnp.exp(-0.5 * values * values) * (1.0 / math.sqrt(2.0 * math.pi))
    return normal_cdf + values * density


def dot(a, b, dims=None):
    if dims is None:
        return jnp.dot(a, b, preferred_element_type=F32)
    return lax.dot_general(a, b, dims, preferred_element_type=F32)


def row_moves(n, digits):
    row = lax.broadcasted_iota(jnp.int32, (n, n), 0)
    col = lax.broadcasted_iota(jnp.int32, (n, n), 1)
    source = jnp.zeros((n, n), jnp.int32)
    for out_stride, size, in_stride in digits:
        digit = (row >> (out_stride.bit_length() - 1)) & (size - 1)
        source = source + (digit << (in_stride.bit_length() - 1))
    return jnp.where(source == col, 1.0, 0.0).astype(BF16)


def turned(n):
    row = lax.broadcasted_iota(jnp.int32, (n, n), 0)
    col = lax.broadcasted_iota(jnp.int32, (n, n), 1)
    sign = jnp.where((row & 4) == 0, 1.0, -1.0)
    return jnp.where((row ^ 4) == col, sign, 0.0).astype(BF16)


def gather_lanes(values, quarter):
    lane = lax.broadcasted_iota(jnp.int32, (values.shape[0], 128), 1) >> 5
    out = None
    for j in range(4):
        block = values[:, 128 * j : 128 * j + 128]
        shift = (32 * (j - quarter)) % 128
        if shift:
            block = pltpu.roll(block, shift, 1)
        out = block if out is None else jnp.where(lane == j, block, out)
    return out


def spectra_kernel(table_ref, fields_ref, pre_ref, cot_ref, out_ref):
    spec_u = dot(table_ref[...], fields_ref[0]).astype(BF16)
    slopes = cot_ref[0].astype(F32) * gelu_slope(pre_ref[0].astype(F32))
    spec_g = dot(table_ref[...], slopes.astype(BF16)).astype(BF16)
    for j in range(4):
        for p in range(2):
            rows = slice(64 * p + 16 * j, 64 * p + 16 * j + 16)
            out_ref[j, 16 * p : 16 * p + 16, :] = spec_g[rows]
            out_ref[j, 32 + 16 * p : 48 + 16 * p, :] = spec_u[rows]


def sum_y_kernel(in_ref, out_ref):
    total = in_ref[0:4].astype(F32)
    for y in range(1, 4):
        total = total + in_ref[4 * y : 4 * y + 4].astype(F32)
    low = total.astype(BF16)
    moves = row_moves(128, [(32, 4, 1), (8, 4, 4), (4, 2, 16), (1, 4, 32)])
    g = dot(moves, low[:, :32].reshape(128, 512))
    u = dot(moves, low[:, 32:].reshape(128, 512))
    for i in range(16):
        both = jnp.concatenate([g[8 * i : 8 * i + 8], u[8 * i : 8 * i + 8]], axis=0)
        out_ref[i] = both.astype(BF16)


def modes_kernel(factor, where_ref, in_ref, w_ref, out_ref, *rest):
    side_refs, chunks = rest[:4], rest[4]
    x, w_mine, zl_mine = where_ref[0], where_ref[1], where_ref[2]
    total = in_ref[0:4].astype(F32)
    for zl in range(1, 4):
        total = total + in_ref[4 * zl : 4 * zl + 4].astype(F32)
    first_mode = (x == 0) & (w_mine == 0) & (zl_mine == 0)
    g = total[:, :8].reshape(32, 512) * jnp.where(first_mode, factor, 2.0 * factor)
    u = total[:, 8:].reshape(32, 512) * factor
    g_low = g.astype(BF16)
    g_turned = dot(turned(32), g_low).astype(BF16)
    grad = dot(g_low, w_ref[0], NT) + dot(g_turned, w_ref[1], NT)
    for w in range(4):
        part = grad[8 * w : 8 * w + 8].astype(BF16)
        for zl in range(4):
            out_ref[4 * zl + w] = part
    for zl in range(4):
        lanes = gather_lanes(g, zl)
        chunks[zl] = jnp.concatenate([lanes[8 * w : 8 * w + 8] for w in range(4)], axis=1)
    for t in range(4):
        chunk = chunks[(zl_mine + t) & 3]
        side_refs[t][...] = jnp.concatenate([u, chunk], axis=0).astype(BF16)


def turn_kernel(where_ref, in_ref, *rest):
    side_refs, out_ref, send_refs, chunks = rest[:4], rest[4], rest[5:9], rest[9]
    y_mine = where_ref[3]
    grad = in_ref[...].astype(F32).reshape(128, 512).astype(BF16)
    grad = dot(row_moves(128, [(32, 4, 1), (16, 2, 4), (4, 4, 8), (1, 4, 32)]), grad)
    for x in range(4):
        part = grad[32 * x : 32 * x + 32].astype(BF16)
        for y in range(4):
            out_ref[4 * y + x] = part
    mine = [ref[32:40, :].astype(F32) for ref in side_refs]
    for y in range(4):
        chunks[y] = jnp.concatenate([gather_lanes(m, y) for m in mine], axis=1)
    for t in range(4):
        for q in range(4):
            send_refs[t][32 * q : 32 * q + 32, :] = side_refs[q][0:32, :]
        send_refs[t][128:136, :] = chunks[(y_mine + t) & 3].astype(BF16)


def weight_kernel(where_ref, *refs):
    in_refs, weight_ref = refs[:4], refs[4]
    zl_mine = where_ref[2]
    g = jnp.concatenate([ref[128:136, :].astype(F32) for ref in in_refs], axis=0)
    g_turned = dot(turned(32), g.astype(BF16))
    lane = lax.broadcasted_iota(jnp.int32, (32, 128), 1)
    for q in range(4):
        one, two = (v[:, 128 * q : 128 * q + 128] for v in (g, g_turned))
        left, right = [], []
        for w in range(4):
            a = pltpu.roll(one, (128 - 32 * w) % 128, 1) if w else one
            b = pltpu.roll(two, (160 - 32 * w) % 128, 1) if w != 1 else two
            left.append(jnp.where(lane < 32, a, b))
            rows = slice(32 * q + 8 * w, 32 * q + 8 * w + 8)
            right += [ref[rows, :].astype(F32) for ref in in_refs]
        left = jnp.concatenate(left, axis=0).astype(BF16)
        right = jnp.concatenate(right, axis=0).astype(BF16)
        grad = dot(left, right, TN)
        ki = (zl_mine - q) & 3
        weight_ref[ki, 0] = grad[0:32]
        weight_ref[ki, 1] = grad[32:64]


def field_kernel(factor, in_ref, table_ref, field_ref):
    modes = jnp.concatenate(
        [in_ref[j, 16 * p : 16 * p + 16, :] for p in range(2) for j in range(4)], axis=0
    )
    field_ref[0] = (dot(table_ref[...], modes) * factor).astype(BF16)


def shifted(value, axis, distance):
    return lax.ppermute(value, axis, [(i, (i + distance) % 4) for i in range(4)])


def shards(fields, pre_act, cotangent, weights):
    points = fields.shape[1]
    total = points * lax.axis_size("y") * lax.axis_size("zl")
    factor = float(total) ** (-0.5)
    x, w, zl, y = (lax.axis_index(name) for name in ("x", "w", "zl", "y"))
    table = make_table(64, points, (y * 4 + zl) * points, total)
    where = jnp.stack([x, w, zl, y]).astype(jnp.int32)
    smem = pl.BlockSpec(memory_space=pltpu.SMEM)
    vmem = pl.BlockSpec(memory_space=pltpu.VMEM)
    params = pltpu.CompilerParams(vmem_limit_bytes=40 * 2**20)

    def block(*shape):
        return jax.ShapeDtypeStruct(shape, BF16)

    half = pl.BlockSpec((1, 512, 256), lambda b, h: (b, 0, h))
    send = pl.pallas_call(
        spectra_kernel,
        grid=(4, 2),
        in_specs=[pl.BlockSpec((128, 512), lambda b, h: (0, 0)), half, half, half],
        out_specs=pl.BlockSpec((4, 64, 256), lambda b, h: (b, 0, h)),
        out_shape=block(16, 64, 512),
        compiler_params=pltpu.CompilerParams(vmem_limit_bytes=SPECTRA_VMEM),
        name="spectra",
    )(table, fields, pre_act, cotangent)
    got = lax.all_to_all(send, FIRST, 0, 0, tiled=True)
    send = pl.pallas_call(
        sum_y_kernel,
        in_specs=[vmem],
        out_specs=vmem,
        out_shape=block(16, 16, 512),
        compiler_params=params,
        name="sum_y",
    )(got)
    got = lax.all_to_all(send, SECOND, 0, 0, tiled=True)
    mine = lax.dynamic_index_in_dim(weights, zl, 0, keepdims=False)
    send, *sides = pl.pallas_call(
        functools.partial(modes_kernel, factor),
        in_specs=[smem, vmem, vmem],
        out_specs=[vmem] * 5,
        out_shape=[block(16, 8, 512)] + [block(40, 512)] * 4,
        scratch_shapes=[pltpu.VMEM((4, 8, 512), F32)],
        compiler_params=params,
        name="modes",
    )(where, got, mine)
    sides = [sides[0]] + [shifted(sides[t], "zl", t) for t in range(1, 4)]
    got = lax.all_to_all(send, SECOND, 0, 0, tiled=True)
    send, *sides = pl.pallas_call(
        turn_kernel,
        in_specs=[smem] + [vmem] * 5,
        out_specs=[vmem] * 5,
        out_shape=[block(16, 32, 512)] + [block(136, 512)] * 4,
        scratch_shapes=[pltpu.VMEM((4, 8, 512), F32)],
        compiler_params=params,
        name="turn",
    )(where, got, *sides)
    sides = [sides[0]] + [shifted(sides[t], "y", t) for t in range(1, 4)]
    got = lax.all_to_all(send, FIRST, 0, 0, tiled=True)
    weight_grad = pl.pallas_call(
        weight_kernel,
        in_specs=[smem] + [vmem] * 4,
        out_specs=vmem,
        out_shape=jax.ShapeDtypeStruct((4, 2, 32, 512), F32),
        compiler_params=params,
        cost_estimate=pl.CostEstimate(
            flops=2**26, bytes_accessed=2**20, transcendentals=0
        ),
        name="weight",
    )(where, *sides)
    field_grad = pl.pallas_call(
        functools.partial(field_kernel, factor),
        grid=(4,),
        in_specs=[
            pl.BlockSpec((4, 32, 512), lambda b: (b, 0, 0)),
            pl.BlockSpec((512, 128), lambda b: (0, 0)),
        ],
        out_specs=pl.BlockSpec((1, 512, 512), lambda b: (b, 0, 0)),
        out_shape=block(4, 512, 512),
        compiler_params=params,
        name="field",
    )(got, lax.optimization_barrier(table).T)
    return field_grad, jnp.swapaxes(weight_grad, 2, 3)


def solution(mesh):
    grid = Mesh(mesh.devices.reshape(4, 4, 4, 4), ("y", "zl", "x", "w"))
    space, mode = ("y", "zl"), ("x", "w")
    whole = P(mode, space, None)
    return jax.shard_map(
        shards,
        mesh=grid,
        in_specs=(whole, whole, whole, P(mode, None, None, None)),
        out_specs=(whole, P(mode, None, None, space)),
        check_vma=False,
    )
```

```python
import functools
import math

import jax
import jax.numpy as jnp
from jax import lax
from jax.experimental import pallas as pl
from jax.experimental.pallas import tpu as pltpu
from jax.sharding import Mesh
from jax.sharding import PartitionSpec as P

F32, BF16 = jnp.float32, jnp.bfloat16
FIRST = ("y", "x")
SECOND = ("zl", "w")
SPECTRA_VMEM = 60 * 2**20
NT = (((1,), (1,)), ((), ()))
TN = (((0,), (0,)), ((), ()))


def table_of(points, rows_are_points, offset):
    shape = (points, 128) if rows_are_points else (128, points)
    point = lax.broadcasted_iota(jnp.int32, shape, 0 if rows_are_points else 1) + offset
    row = lax.broadcasted_iota(jnp.int32, shape, 1 if rows_are_points else 0)
    phase = ((row & 63) * point + ((row >> 6) << 11)) & 8191
    quadrant = (phase + 1024) >> 11
    angle = (phase - (quadrant << 11)).astype(F32) * (2.0 * math.pi / 8192.0)
    square = angle * angle
    sine = 1.0 / 362880.0
    for c in (-1.0 / 5040.0, 1.0 / 120.0, -1.0 / 6.0, 1.0):
        sine = sine * square + c
    sine = sine * angle
    cosine = -1.0 / 3628800.0
    for c in (1.0 / 40320.0, -1.0 / 720.0, 1.0 / 24.0, -0.5, 1.0):
        cosine = cosine * square + c
    value = jnp.where((quadrant & 1) == 0, cosine, sine)
    negative = ((quadrant + 1) & 2) != 0
    return jnp.where(negative, -value, value).astype(BF16)


def gelu_slope(values):
    normal_cdf = 0.5 * (1.0 + lax.erf(values * (1.0 / math.sqrt(2.0))))
    density = jnp.exp(-0.5 * values * values) * (1.0 / math.sqrt(2.0 * math.pi))
    return normal_cdf + values * density


def dot(a, b, dims=None):
    if dims is None:
        return jnp.dot(a, b, preferred_element_type=F32)
    return lax.dot_general(a, b, dims, preferred_element_type=F32)


def row_moves(n, digits):
    row = lax.broadcasted_iota(jnp.int32, (n, n), 0)
    col = lax.broadcasted_iota(jnp.int32, (n, n), 1)
    source = jnp.zeros((n, n), jnp.int32)
    for out_stride, size, in_stride in digits:
        digit = (row >> (out_stride.bit_length() - 1)) & (size - 1)
        source = source + (digit << (in_stride.bit_length() - 1))
    return jnp.where(source == col, 1.0, 0.0).astype(BF16)


def turned(n):
    row = lax.broadcasted_iota(jnp.int32, (n, n), 0)
    col = lax.broadcasted_iota(jnp.int32, (n, n), 1)
    sign = jnp.where((row & 4) == 0, 1.0, -1.0)
    return jnp.where((row ^ 4) == col, sign, 0.0).astype(BF16)


def gather_lanes(values, quarter):
    lane = lax.broadcasted_iota(jnp.int32, (values.shape[0], 128), 1) >> 5
    out = None
    for j in range(4):
        block = values[:, 128 * j : 128 * j + 128]
        shift = (32 * (j - quarter)) % 128
        if shift:
            block = pltpu.roll(block, shift, 1)
        out = block if out is None else jnp.where(lane == j, block, out)
    return out


def spectra_kernel(fields_hbm, pre_hbm, cot_hbm, out_hbm, fields, pre, cot, out_ref, table, sems, out_sems):
    def copies(b):
        return [
            pltpu.make_async_copy(hbm.at[b], vmem.at[b], sems.at[i, b])
            for i, (hbm, vmem) in enumerate(((pre_hbm, pre), (cot_hbm, cot), (fields_hbm, fields)))
        ]

    def copy_out(b):
        rows = pl.ds(4 * b, 4)
        return pltpu.make_async_copy(out_ref.at[rows], out_hbm.at[rows], out_sems.at[b])

    for b in range(4):
        for copy in copies(b):
            copy.start()
    points = table.shape[1]
    table[...] = table_of(points, False, (lax.axis_index("y") * 4 + lax.axis_index("zl")) * points)

    def one(b, _):
        for copy in copies(b):
            copy.wait()
        for h in range(2):
            lanes = slice(256 * h, 256 * h + 256)
            slopes = cot[b, :, lanes].astype(F32) * gelu_slope(pre[b, :, lanes].astype(F32))
            spec_g = dot(table[...], slopes.astype(BF16)).astype(BF16)
            spec_u = dot(table[...], fields[b, :, lanes]).astype(BF16)
            for j in range(4):
                for p in range(2):
                    rows = slice(64 * p + 16 * j, 64 * p + 16 * j + 16)
                    out_ref[4 * b + j, 16 * p : 16 * p + 16, lanes] = spec_g[rows]
                    out_ref[4 * b + j, 32 + 16 * p : 48 + 16 * p, lanes] = spec_u[rows]
        copy_out(b).start()
        return 0

    lax.fori_loop(0, 4, one, 0)
    for b in range(4):
        copy_out(b).wait()


def sum_y_kernel(in_ref, out_ref):
    total = in_ref[0:4].astype(F32)
    for y in range(1, 4):
        total = total + in_ref[4 * y : 4 * y + 4].astype(F32)
    low = total.astype(BF16)
    moves = row_moves(128, [(32, 4, 1), (8, 4, 4), (4, 2, 16), (1, 4, 32)])
    g = dot(moves, low[:, :32].reshape(128, 512))
    u = dot(moves, low[:, 32:].reshape(128, 512))
    for i in range(16):
        both = jnp.concatenate([g[8 * i : 8 * i + 8], u[8 * i : 8 * i + 8]], axis=0)
        out_ref[i] = both.astype(BF16)


def modes_kernel(factor, in_ref, w_ref, out_ref, *rest):
    side_refs, chunks = rest[:4], rest[4]
    x, w_mine, zl_mine, y_mine = (lax.axis_index(name) for name in ("x", "w", "zl", "y"))
    total = in_ref[0:4].astype(F32)
    for zl in range(1, 4):
        total = total + in_ref[4 * zl : 4 * zl + 4].astype(F32)
    first_mode = (x == 0) & (w_mine == 0) & (zl_mine == 0)
    g = total[:, :8].reshape(32, 512) * jnp.where(first_mode, factor, 2.0 * factor)
    u = total[:, 8:].reshape(32, 512) * factor
    g_low = g.astype(BF16)
    g_turned = dot(turned(32), g_low).astype(BF16)
    grad = dot(g_low, w_ref[0], NT) + dot(g_turned, w_ref[1], NT)
    for w in range(4):
        part = grad[8 * w : 8 * w + 8].astype(BF16)
        for zl in range(4):
            out_ref[4 * zl + w] = part
    for y in range(4):
        lanes = slice(128 * y, 128 * y + 128)
        chunks[y] = jnp.concatenate([g[8 * w : 8 * w + 8, lanes] for w in range(4)], axis=1)
    for t in range(4):
        chunk = chunks[(y_mine + t) & 3]
        side_refs[t][...] = jnp.concatenate([u, chunk], axis=0).astype(BF16)


def turn_kernel(in_ref, *rest):
    side_refs, out_ref, send_refs, chunks = rest[:4], rest[4], rest[5:9], rest[9]
    grad = in_ref[...].astype(F32).reshape(128, 512).astype(BF16)
    grad = dot(row_moves(128, [(32, 4, 1), (16, 2, 4), (4, 4, 8), (1, 4, 32)]), grad)
    for x in range(4):
        part = grad[32 * x : 32 * x + 32].astype(BF16)
        for y in range(4):
            out_ref[4 * y + x] = part
    mine = [ref[32:40, :].astype(F32) for ref in side_refs]
    for zl in range(4):
        chunks[zl] = jnp.concatenate([gather_lanes(m, zl) for m in mine], axis=1)
    for t in range(4):
        for q in range(4):
            send_refs[t][32 * q : 32 * q + 32, :] = side_refs[q][0:32, :]
        send_refs[t][128:136, :] = chunks[(lax.axis_index("zl") + t) & 3].astype(BF16)


def weight_kernel(done_ref, *refs):
    in_refs, weight_ref = refs[:4], refs[4]
    g = jnp.concatenate([ref[128:136, :].astype(F32) for ref in in_refs], axis=0)
    g_turned = dot(turned(32), g.astype(BF16))
    lane = lax.broadcasted_iota(jnp.int32, (32, 128), 1)
    left = []
    for q in range(4):
        one, two = (v[:, 128 * q : 128 * q + 128] for v in (g, g_turned))
        for w in range(4):
            a = pltpu.roll(one, (128 - 32 * w) % 128, 1) if w else one
            b = pltpu.roll(two, (160 - 32 * w) % 128, 1) if w != 1 else two
            left.append(jnp.where(lane < 32, a, b))
    for t in range(4):
        mine = jnp.concatenate([rows[8 * t : 8 * t + 8] for rows in left], axis=0)
        grad = dot(mine.astype(BF16), in_refs[t][0:128, :], TN)
        ki = (lax.axis_index("zl") - t) & 3
        weight_ref[ki, 0] = grad[0:32]
        weight_ref[ki, 1] = grad[32:64]


def field_kernel(factor, in_ref, field_ref, done_ref, table):
    @pl.when(pl.program_id(0) == 0)
    def _():
        done_ref[...] = jnp.zeros_like(done_ref)
        points = table.shape[0]
        offset = (lax.axis_index("y") * 4 + lax.axis_index("zl")) * points
        table[...] = table_of(points, True, offset)

    modes = jnp.concatenate(
        [in_ref[j, 16 * p : 16 * p + 16, :] for p in range(2) for j in range(4)], axis=0
    )
    field_ref[0] = (dot(table[...], modes) * factor).astype(BF16)


def shifted(value, axis, distance):
    return lax.ppermute(value, axis, [(i, (i + distance) % 4) for i in range(4)])


def shards(fields, pre_act, cotangent, weights):
    total = fields.shape[1] * lax.axis_size("y") * lax.axis_size("zl")
    factor = float(total) ** (-0.5)
    vmem = pl.BlockSpec(memory_space=pltpu.VMEM)
    hbm = pl.BlockSpec(memory_space=pltpu.HBM)
    params = pltpu.CompilerParams(vmem_limit_bytes=40 * 2**20)

    def block(*shape):
        return jax.ShapeDtypeStruct(shape, BF16)

    send = pl.pallas_call(
        spectra_kernel,
        in_specs=[hbm] * 3,
        out_specs=hbm,
        out_shape=block(16, 64, 512),
        scratch_shapes=[pltpu.VMEM((4, 512, 512), BF16)] * 3
        + [pltpu.VMEM((16, 64, 512), BF16), pltpu.VMEM((128, 512), BF16)]
        + [pltpu.SemaphoreType.DMA((3, 4)), pltpu.SemaphoreType.DMA((4,))],
        compiler_params=pltpu.CompilerParams(vmem_limit_bytes=SPECTRA_VMEM),
        name="spectra",
    )(fields, pre_act, cotangent)
    got = lax.all_to_all(send, FIRST, 0, 0, tiled=True)
    send = pl.pallas_call(
        sum_y_kernel,
        in_specs=[vmem],
        out_specs=vmem,
        out_shape=block(16, 16, 512),
        compiler_params=params,
        name="sum_y",
    )(got)
    got = lax.all_to_all(send, SECOND, 0, 0, tiled=True)
    mine = lax.dynamic_index_in_dim(weights, lax.axis_index("zl"), 0, keepdims=False)
    send, *sides = pl.pallas_call(
        functools.partial(modes_kernel, factor),
        in_specs=[vmem, vmem],
        out_specs=[vmem] * 5,
        out_shape=[block(16, 8, 512)] + [block(40, 512)] * 4,
        scratch_shapes=[pltpu.VMEM((4, 8, 512), F32)],
        compiler_params=params,
        name="modes",
    )(got, mine)
    sides = [sides[0]] + [shifted(sides[t], "y", t) for t in range(1, 4)]
    got = lax.all_to_all(send, SECOND, 0, 0, tiled=True)
    send, *sides = pl.pallas_call(
        turn_kernel,
        in_specs=[vmem] * 5,
        out_specs=[vmem] * 5,
        out_shape=[block(16, 32, 512)] + [block(136, 512)] * 4,
        scratch_shapes=[pltpu.VMEM((4, 8, 512), F32)],
        compiler_params=params,
        name="turn",
    )(got, *sides)
    sides = [sides[0]] + [shifted(sides[t], "zl", t) for t in range(1, 4)]
    got = lax.all_to_all(send, FIRST, 0, 0, tiled=True)
    field_grad, done = pl.pallas_call(
        functools.partial(field_kernel, factor),
        grid=(4,),
        in_specs=[pl.BlockSpec((4, 32, 512), lambda b: (b, 0, 0))],
        out_specs=[
            pl.BlockSpec((1, 512, 512), lambda b: (b, 0, 0)),
            pl.BlockSpec((8, 128), lambda b: (0, 0)),
        ],
        out_shape=[block(4, 512, 512), jax.ShapeDtypeStruct((8, 128), F32)],
        scratch_shapes=[pltpu.VMEM((512, 128), BF16)],
        compiler_params=params,
        name="field",
    )(got)
    weight_grad = pl.pallas_call(
        weight_kernel,
        in_specs=[vmem] * 5,
        out_specs=vmem,
        out_shape=jax.ShapeDtypeStruct((4, 2, 32, 512), F32),
        compiler_params=params,
        name="weight",
    )(done, *sides)
    return field_grad, jnp.swapaxes(weight_grad, 2, 3)


def solution(mesh):
    grid = Mesh(mesh.devices.reshape(4, 4, 4, 4), ("y", "zl", "x", "w"))
    space, mode = ("y", "zl"), ("x", "w")
    whole = P(mode, space, None)
    return jax.shard_map(
        shards,
        mesh=grid,
        in_specs=(whole, whole, whole, P(mode, None, None, None)),
        out_specs=(whole, P(mode, None, None, space)),
        check_vma=False,
    )
```

```python
import functools
import math

import jax
import jax.numpy as jnp
from jax import lax
from jax.experimental import pallas as pl
from jax.experimental.pallas import tpu as pltpu
from jax.sharding import Mesh
from jax.sharding import PartitionSpec as P

F32, BF16 = jnp.float32, jnp.bfloat16
OTHERS = ("x", "w", "zl")
SPECTRA_VMEM = 60 * 2**20
NT = (((1,), (1,)), ((), ()))
TN = (((0,), (0,)), ((), ()))


def table_of(points, rows_are_points, offset):
    shape = (points, 128) if rows_are_points else (128, points)
    point = lax.broadcasted_iota(jnp.int32, shape, 0 if rows_are_points else 1) + offset
    row = lax.broadcasted_iota(jnp.int32, shape, 1 if rows_are_points else 0)
    phase = ((row & 63) * point + ((row >> 6) << 11)) & 8191
    quadrant = (phase + 1024) >> 11
    angle = (phase - (quadrant << 11)).astype(F32) * (2.0 * math.pi / 8192.0)
    square = angle * angle
    sine = 1.0 / 362880.0
    for c in (-1.0 / 5040.0, 1.0 / 120.0, -1.0 / 6.0, 1.0):
        sine = sine * square + c
    sine = sine * angle
    cosine = -1.0 / 3628800.0
    for c in (1.0 / 40320.0, -1.0 / 720.0, 1.0 / 24.0, -0.5, 1.0):
        cosine = cosine * square + c
    value = jnp.where((quadrant & 1) == 0, cosine, sine)
    negative = ((quadrant + 1) & 2) != 0
    return jnp.where(negative, -value, value).astype(BF16)


def gelu_slope(values):
    normal_cdf = 0.5 * (1.0 + lax.erf(values * (1.0 / math.sqrt(2.0))))
    density = jnp.exp(-0.5 * values * values) * (1.0 / math.sqrt(2.0 * math.pi))
    return normal_cdf + values * density


def dot(a, b, dims=None):
    if dims is None:
        return jnp.dot(a, b, preferred_element_type=F32)
    return lax.dot_general(a, b, dims, preferred_element_type=F32)


def row_moves(shape, digits, only=(), base=0):
    row = lax.broadcasted_iota(jnp.int32, shape, 0)
    col = lax.broadcasted_iota(jnp.int32, shape, 1)
    source = jnp.full(shape, base, jnp.int32)
    for out_stride, size, in_stride in digits:
        digit = (row >> (out_stride.bit_length() - 1)) & (size - 1)
        source = source + (digit << (in_stride.bit_length() - 1))
    for out_stride, size, wanted in only:
        digit = (row >> (out_stride.bit_length() - 1)) & (size - 1)
        source = jnp.where(digit == wanted, source, -1)
    return jnp.where(source == col, 1.0, 0.0).astype(BF16)


def turned(n):
    row = lax.broadcasted_iota(jnp.int32, (n, n), 0)
    col = lax.broadcasted_iota(jnp.int32, (n, n), 1)
    sign = jnp.where((row & 4) == 0, 1.0, -1.0)
    return jnp.where((row ^ 4) == col, sign, 0.0).astype(BF16)


def gather_lanes(values, quarter):
    lane = lax.broadcasted_iota(jnp.int32, (values.shape[0], 128), 1) >> 5
    out = None
    for j in range(4):
        block = values[:, 128 * j : 128 * j + 128]
        shift = (32 * (j - quarter)) % 128
        if shift:
            block = pltpu.roll(block, shift, 1)
        out = block if out is None else jnp.where(lane == j, block, out)
    return out


def spectra_kernel(steps, fields_hbm, pre_hbm, cot_hbm, _, *rest):
    out_refs, (fields, pre, cot, table, sems) = rest[: len(steps)], rest[len(steps) :]
    y = lax.axis_index("y")

    def copies(i):
        b = (y + steps[i]) & 3
        return [
            pltpu.make_async_copy(hbm.at[b], vmem.at[i], sems.at[n, i])
            for n, (hbm, vmem) in enumerate(((pre_hbm, pre), (cot_hbm, cot), (fields_hbm, fields)))
        ]

    for i in range(len(steps)):
        for copy in copies(i):
            copy.start()
    points = table.shape[1]
    table[...] = table_of(points, False, (y * 4 + lax.axis_index("zl")) * points)
    for i in range(len(steps)):
        for copy in copies(i):
            copy.wait()
        for h in range(2):
            lanes = slice(256 * h, 256 * h + 256)
            slopes = cot[i, :, lanes].astype(F32) * gelu_slope(pre[i, :, lanes].astype(F32))
            out_refs[i][0:128, lanes] = dot(table[...], slopes.astype(BF16)).astype(BF16)
            out_refs[i][128:256, lanes] = dot(table[...], fields[i, :, lanes]).astype(BF16)


def sum_y_kernel(*refs):
    in_refs, out_ref = refs[:4], refs[4]
    total = in_refs[0][...].astype(F32)
    for ref in in_refs[1:]:
        total = total + ref[...].astype(F32)
    low = total.astype(BF16)
    out = None
    for h in range(2):
        moves = row_moves((512, 256), [(8, 64, 1), (2, 2, 128), (1, 2, 64)], [(4, 2, h)])
        part = dot(moves, low[:, 256 * h : 256 * h + 256])
        out = part if out is None else out + part
    out_ref[...] = out.reshape(64, 8, 256).astype(BF16)


def modes_kernel(factor, in_ref, w_ref, out_ref, *rest):
    side_refs, chunks = rest[:4], rest[4]
    x, w_mine, zl_mine, y_mine = (lax.axis_index(name) for name in ("x", "w", "zl", "y"))
    total = jnp.sum(in_ref[...].astype(F32).reshape(16, 4, 8, 256), axis=1).reshape(128, 256)
    first_mode = (x == 0) & (w_mine == 0) & (zl_mine == 0)
    is_u = (lax.broadcasted_iota(jnp.int32, (128, 256), 0) & 2) != 0
    g_scale = jnp.where(first_mode, factor, 2.0 * factor)
    low = (total * jnp.where(is_u, factor, g_scale)).astype(BF16)
    digits = [(32, 2, 2), (8, 4, 8), (4, 2, 1), (1, 4, 32)]
    both = [dot(row_moves((64, 128), digits, base=4 * h), low) for h in range(2)]
    both = jnp.concatenate(both, axis=1)
    g, u = both[:32], both[32:]
    g_low = g.astype(BF16)
    g_turned = dot(turned(32), g_low).astype(BF16)
    grad = (dot(g_low, w_ref[0], NT) + dot(g_turned, w_ref[1], NT)).astype(BF16)
    out = None
    for q in range(4):
        moves = row_moves((128, 32), [(32, 4, 1), (8, 4, 8), (1, 2, 4)], [(2, 4, q)])
        part = dot(moves, grad[:, 128 * q : 128 * q + 128])
        out = part if out is None else out + part
    out = out.reshape(16, 8, 128).astype(BF16)
    for zl in range(4):
        out_ref[:, zl] = out
    for y in range(4):
        lanes = slice(128 * y, 128 * y + 128)
        chunks[y] = jnp.concatenate([g[8 * w : 8 * w + 8, lanes] for w in range(4)], axis=1)
    for t in range(4):
        chunk = chunks[(y_mine + t) & 3]
        side_refs[t][...] = jnp.concatenate([u, chunk], axis=0).astype(BF16)


def relay_kernel(*refs):
    side_refs, send_refs, chunks = refs[:4], refs[4:8], refs[8]
    mine = [ref[32:40, :].astype(F32) for ref in side_refs]
    for zl in range(4):
        chunks[zl] = jnp.concatenate([gather_lanes(m, zl) for m in mine], axis=1)
    for t in range(4):
        for q in range(4):
            send_refs[t][32 * q : 32 * q + 32, :] = side_refs[q][0:32, :]
        send_refs[t][128:136, :] = chunks[(lax.axis_index("zl") + t) & 3].astype(BF16)


def weight_kernel(*refs):
    in_refs, weight_ref = refs[:4], refs[4]
    g = jnp.concatenate([ref[128:136, :].astype(F32) for ref in in_refs], axis=0)
    g_turned = dot(turned(32), g.astype(BF16))
    lane = lax.broadcasted_iota(jnp.int32, (32, 128), 1)
    left = []
    for q in range(4):
        one, two = (v[:, 128 * q : 128 * q + 128] for v in (g, g_turned))
        for w in range(4):
            a = pltpu.roll(one, (128 - 32 * w) % 128, 1) if w else one
            b = pltpu.roll(two, (160 - 32 * w) % 128, 1) if w != 1 else two
            left.append(jnp.where(lane < 32, a, b))
    for t in range(4):
        mine = jnp.concatenate([rows[8 * t : 8 * t + 8] for rows in left], axis=0)
        grad = dot(mine.astype(BF16), in_refs[t][0:128, :], TN)
        ki = (lax.axis_index("zl") - t) & 3
        weight_ref[ki, 0] = grad[0:32]
        weight_ref[ki, 1] = grad[32:64]


def field_kernel(factor, step, in_ref, *rest):
    if step == 0:
        field_hbm, table_ref, out, sem = rest
        points = table_ref.shape[0]
        offset = (lax.axis_index("y") * 4 + lax.axis_index("zl")) * points
        table_ref[...] = table_of(points, True, offset)
    else:
        table_ref, _, field_hbm, out, sem = rest
    blocks = in_ref[...].astype(F32).reshape(512, 128).astype(BF16)
    b = (lax.axis_index("y") - step) & 3
    copies = []
    for h in range(2):
        modes = []
        for q in (2 * h, 2 * h + 1):
            row = lax.broadcasted_iota(jnp.int32, (128, 512), 0)
            col = lax.broadcasted_iota(jnp.int32, (128, 512), 1)
            source = ((row & 63) << 3) + (row >> 6) + 2 * q
            modes.append(dot(jnp.where(source == col, 1.0, 0.0).astype(BF16), blocks))
        modes = jnp.concatenate(modes, axis=1).astype(BF16)
        out[h] = (dot(table_ref[...], modes) * factor).astype(BF16)
        lanes = slice(256 * h, 256 * h + 256)
        copies.append(pltpu.make_async_copy(out.at[h], field_hbm.at[b, :, lanes], sem.at[h]))
        copies[-1].start()
    for copy in copies:
        copy.wait()


def shifted(value, axis, distance):
    return lax.ppermute(value, axis, [(i, (i + distance) % 4) for i in range(4)])


def cost(flops, bytes_accessed):
    return pl.CostEstimate(flops=flops, bytes_accessed=bytes_accessed, transcendentals=0)


def shards(fields, pre_act, cotangent, weights):
    total = fields.shape[1] * lax.axis_size("y") * lax.axis_size("zl")
    factor = float(total) ** (-0.5)
    vmem = pl.BlockSpec(memory_space=pltpu.VMEM)
    hbm = pl.BlockSpec(memory_space=pltpu.HBM)
    params = pltpu.CompilerParams(vmem_limit_bytes=40 * 2**20)

    def block(*shape):
        return jax.ShapeDtypeStruct(shape, BF16)

    def spectra(steps, after):
        n = len(steps)
        return pl.pallas_call(
            functools.partial(spectra_kernel, steps),
            in_specs=[hbm] * 4,
            out_specs=[vmem] * n,
            out_shape=[block(256, 512)] * n,
            scratch_shapes=[pltpu.VMEM((n, 512, 512), BF16)] * 3
            + [pltpu.VMEM((128, 512), BF16), pltpu.SemaphoreType.DMA((3, n))],
            compiler_params=pltpu.CompilerParams(vmem_limit_bytes=SPECTRA_VMEM),
            cost_estimate=cost(2**28 * n, 2**22 * n),
            name="spectra",
        )(fields, pre_act, cotangent, after)

    (two,) = spectra((2,), fields)
    one, three = spectra((1, 3), two)
    (own,) = spectra((0,), one)
    one, two, three = shifted(one, "y", 1), shifted(two, "y", 2), shifted(three, "y", 3)
    send = pl.pallas_call(
        sum_y_kernel,
        in_specs=[vmem] * 4,
        out_specs=vmem,
        out_shape=block(64, 8, 256),
        compiler_params=params,
        name="sum_y",
    )(own, one, two, three)
    got = lax.all_to_all(send, OTHERS, 0, 0, tiled=True)
    mine = lax.dynamic_index_in_dim(weights, lax.axis_index("zl"), 0, keepdims=False)
    send, *sides = pl.pallas_call(
        functools.partial(modes_kernel, factor),
        in_specs=[vmem, vmem],
        out_specs=[vmem] * 5,
        out_shape=[block(16, 4, 8, 128)] + [block(40, 512)] * 4,
        scratch_shapes=[pltpu.VMEM((4, 8, 512), F32)],
        compiler_params=params,
        name="modes",
    )(got, mine)
    sides = [sides[0]] + [shifted(sides[t], "y", t) for t in range(1, 4)]
    got = lax.all_to_all(send.reshape(64, 8, 128), OTHERS, 0, 0, tiled=True)
    sides = pl.pallas_call(
        relay_kernel,
        in_specs=[vmem] * 4,
        out_specs=[vmem] * 4,
        out_shape=[block(136, 512)] * 4,
        scratch_shapes=[pltpu.VMEM((4, 8, 512), F32)],
        compiler_params=params,
        cost_estimate=cost(2**26, 2**20),
        name="relay",
    )(*sides)
    sides = [sides[0]] + [shifted(sides[t], "zl", t) for t in range(1, 4)]
    weight_grad = pl.pallas_call(
        weight_kernel,
        in_specs=[vmem] * 4,
        out_specs=vmem,
        out_shape=jax.ShapeDtypeStruct((4, 2, 32, 512), F32),
        compiler_params=params,
        cost_estimate=cost(2**27, 2**21),
        name="weight",
    )(*sides)
    scratch = [pltpu.VMEM((2, 512, 256), BF16), pltpu.SemaphoreType.DMA((2,))]
    received = {t: shifted(got, "y", t) for t in (2, 1, 3)}
    field_grad, table = pl.pallas_call(
        functools.partial(field_kernel, factor, 0),
        in_specs=[vmem],
        out_specs=[hbm, vmem],
        out_shape=[block(4, 512, 512), block(512, 128)],
        scratch_shapes=scratch,
        compiler_params=params,
        cost_estimate=cost(2**27, 2**20),
        name="field",
    )(got)
    for t in (1, 3, 2):
        field_grad = pl.pallas_call(
            functools.partial(field_kernel, factor, t),
            in_specs=[vmem, vmem, hbm],
            out_specs=hbm,
            out_shape=block(4, 512, 512),
            scratch_shapes=scratch,
            input_output_aliases={2: 0},
            compiler_params=params,
            cost_estimate=cost(2**27, 2**20),
            name="field",
        )(received[t], table, field_grad)
    return field_grad, jnp.swapaxes(weight_grad, 2, 3)


def solution(mesh):
    grid = Mesh(mesh.devices.reshape(4, 4, 4, 4), ("y", "zl", "x", "w"))
    space, mode = ("y", "zl"), ("x", "w")
    whole = P(mode, space, None)
    return jax.shard_map(
        shards,
        mesh=grid,
        in_specs=(whole, whole, whole, P(mode, None, None, None)),
        out_specs=(whole, P(mode, None, None, space)),
        check_vma=False,
    )
```

```python
import functools
import math

import jax
import jax.numpy as jnp
from jax import lax
from jax.experimental import pallas as pl
from jax.experimental.pallas import tpu as pltpu
from jax.sharding import Mesh
from jax.sharding import PartitionSpec as P

F32, BF16 = jnp.float32, jnp.bfloat16
OTHERS = ("x", "w", "zl")
SPECTRA_VMEM = 60 * 2**20
NT = (((1,), (1,)), ((), ()))
TN = (((0,), (0,)), ((), ()))


def table_of(points, rows_are_points, offset):
    shape = (points, 128) if rows_are_points else (128, points)
    point = lax.broadcasted_iota(jnp.int32, shape, 0 if rows_are_points else 1) + offset
    row = lax.broadcasted_iota(jnp.int32, shape, 1 if rows_are_points else 0)
    phase = ((row & 63) * point + ((row >> 6) << 11)) & 8191
    quadrant = (phase + 1024) >> 11
    angle = (phase - (quadrant << 11)).astype(F32) * (2.0 * math.pi / 8192.0)
    square = angle * angle
    sine = 1.0 / 362880.0
    for c in (-1.0 / 5040.0, 1.0 / 120.0, -1.0 / 6.0, 1.0):
        sine = sine * square + c
    sine = sine * angle
    cosine = -1.0 / 3628800.0
    for c in (1.0 / 40320.0, -1.0 / 720.0, 1.0 / 24.0, -0.5, 1.0):
        cosine = cosine * square + c
    value = jnp.where((quadrant & 1) == 0, cosine, sine)
    negative = ((quadrant + 1) & 2) != 0
    return jnp.where(negative, -value, value).astype(BF16)


def gelu_slope(values):
    normal_cdf = 0.5 * (1.0 + lax.erf(values * (1.0 / math.sqrt(2.0))))
    density = jnp.exp(-0.5 * values * values) * (1.0 / math.sqrt(2.0 * math.pi))
    return normal_cdf + values * density


def dot(a, b, dims=None):
    if dims is None:
        return jnp.dot(a, b, preferred_element_type=F32)
    return lax.dot_general(a, b, dims, preferred_element_type=F32)


def row_moves(shape, digits, only=(), base=0):
    row = lax.broadcasted_iota(jnp.int32, shape, 0)
    col = lax.broadcasted_iota(jnp.int32, shape, 1)
    source = jnp.full(shape, base, jnp.int32)
    for out_stride, size, in_stride in digits:
        digit = (row >> (out_stride.bit_length() - 1)) & (size - 1)
        source = source + (digit << (in_stride.bit_length() - 1))
    for out_stride, size, wanted in only:
        digit = (row >> (out_stride.bit_length() - 1)) & (size - 1)
        source = jnp.where(digit == wanted, source, -1)
    return jnp.where(source == col, 1.0, 0.0).astype(BF16)


def turned(n):
    row = lax.broadcasted_iota(jnp.int32, (n, n), 0)
    col = lax.broadcasted_iota(jnp.int32, (n, n), 1)
    sign = jnp.where((row & 4) == 0, 1.0, -1.0)
    return jnp.where((row ^ 4) == col, sign, 0.0).astype(BF16)


def spectra_kernel(steps, fields_hbm, pre_hbm, cot_hbm, _, *rest):
    out_refs, (fields, pre, cot, table, sems) = rest[: len(steps)], rest[len(steps) :]
    y = lax.axis_index("y")

    def copies(i, h):
        b = (y + steps[i]) & 3
        at = slice(256 * h, 256 * h + 256)
        return [
            pltpu.make_async_copy(hbm.at[b, :, at], vmem.at[i, :, at], sems.at[n, i, h])
            for n, (hbm, vmem) in enumerate(((pre_hbm, pre), (cot_hbm, cot), (fields_hbm, fields)))
        ]

    for i in range(len(steps)):
        for h in range(2):
            for copy in copies(i, h):
                copy.start()
    points = table.shape[1]
    table[...] = table_of(points, False, (y * 4 + lax.axis_index("zl")) * points)
    for i in range(len(steps)):
        for h in range(2):
            for copy in copies(i, h):
                copy.wait()
            lanes = slice(256 * h, 256 * h + 256)
            slopes = cot[i, :, lanes].astype(F32) * gelu_slope(pre[i, :, lanes].astype(F32))
            out_refs[i][0:128, lanes] = dot(table[...], slopes.astype(BF16)).astype(BF16)
            out_refs[i][128:256, lanes] = dot(table[...], fields[i, :, lanes]).astype(BF16)


def sum_y_kernel(own_hbm, one_ref, two_ref, three_ref, out_ref, own, sem):
    copy = pltpu.make_async_copy(own_hbm, own, sem)
    copy.start()
    total = one_ref[...].astype(F32) + two_ref[...].astype(F32) + three_ref[...].astype(F32)
    copy.wait()
    low = (total + own[...].astype(F32)).astype(BF16)
    out = None
    for h in range(2):
        moves = row_moves((512, 256), [(8, 64, 1), (2, 2, 128), (1, 2, 64)], [(4, 2, h)])
        part = dot(moves, low[:, 256 * h : 256 * h + 256])
        out = part if out is None else out + part
    out_ref[...] = out.reshape(64, 8, 256).astype(BF16)


def modes_kernel(factor, in_ref, w_ref, out_ref, *rest):
    side_refs, chunks = rest[:4], rest[4]
    x, w_mine, zl_mine, y_mine = (lax.axis_index(name) for name in ("x", "w", "zl", "y"))
    total = jnp.sum(in_ref[...].astype(F32).reshape(16, 4, 8, 256), axis=1).reshape(128, 256)
    first_mode = (x == 0) & (w_mine == 0) & (zl_mine == 0)
    is_u = (lax.broadcasted_iota(jnp.int32, (128, 256), 0) & 2) != 0
    g_scale = jnp.where(first_mode, factor, 2.0 * factor)
    low = (total * jnp.where(is_u, factor, g_scale)).astype(BF16)
    digits = [(32, 2, 2), (8, 4, 8), (4, 2, 1), (1, 4, 32)]
    both = [dot(row_moves((64, 128), digits, base=4 * h), low) for h in range(2)]
    both = jnp.concatenate(both, axis=1)
    g, u = both[:32], both[32:]
    g_low = g.astype(BF16)
    g_turned = dot(turned(32), g_low).astype(BF16)
    grad = (dot(g_low, w_ref[0], NT) + dot(g_turned, w_ref[1], NT)).astype(BF16)
    out = None
    for q in range(4):
        moves = row_moves((128, 32), [(32, 4, 1), (8, 4, 8), (1, 2, 4)], [(2, 4, q)])
        part = dot(moves, grad[:, 128 * q : 128 * q + 128])
        out = part if out is None else out + part
    out = out.reshape(16, 8, 128).astype(BF16)
    for zl in range(4):
        out_ref[:, zl] = out
    for y in range(4):
        lanes = slice(128 * y, 128 * y + 128)
        chunks[y] = jnp.concatenate([g[8 * w : 8 * w + 8, lanes] for w in range(4)], axis=1)
    for t in range(4):
        chunk = chunks[(y_mine + t) & 3]
        side_refs[t][...] = jnp.concatenate([u, chunk], axis=0).astype(BF16)


def weight_kernel(*refs):
    in_refs, own_ref, send_refs, result = refs[:4], refs[4], refs[5:8], refs[8]
    u = jnp.concatenate([ref[0:32, :] for ref in in_refs], axis=0)
    g = jnp.concatenate(
        [ref[32:40, 128 * w : 128 * w + 128].astype(F32) for ref in in_refs for w in range(4)],
        axis=0,
    ).astype(BF16)
    both = jnp.concatenate([g, dot(turned(128), g).astype(BF16)], axis=1)
    result[...] = dot(both, u, TN).reshape(2, 4, 32, 512)
    zl_mine = lax.axis_index("zl")
    own_ref[...] = result[:, zl_mine]
    for t in range(1, 4):
        send_refs[t - 1][...] = result[:, (zl_mine + t) & 3].reshape(64, 512).astype(BF16)


def place_kernel(_, own_ref, *refs):
    weight_ref = refs[3]
    zl_mine = lax.axis_index("zl")
    weight_ref[zl_mine] = own_ref[...]
    for t in range(1, 4):
        weight_ref[(zl_mine - t) & 3] = refs[t - 1][...].astype(F32).reshape(2, 32, 512)


def field_kernel(factor, step, in_ref, *rest):
    if step == 0:
        field_hbm, table_ref, rows, out, sem = rest
        points = table_ref.shape[0]
        offset = (lax.axis_index("y") * 4 + lax.axis_index("zl")) * points
        table_ref[...] = table_of(points, True, offset)
    else:
        table_ref, _, field_hbm, rows, out, sem = rest
    rows[...] = in_ref[...].astype(F32).reshape(512, 128)
    b = (lax.axis_index("y") - step) & 3
    copies = []
    for h in range(2):
        modes = [
            jnp.concatenate([rows[pl.ds(2 * q + p, 64, stride=8), :] for p in range(2)], axis=0)
            for q in (2 * h, 2 * h + 1)
        ]
        modes = jnp.concatenate(modes, axis=1).astype(BF16)
        out[h] = (dot(table_ref[...], modes) * factor).astype(BF16)
        lanes = slice(256 * h, 256 * h + 256)
        copies.append(pltpu.make_async_copy(out.at[h], field_hbm.at[b, :, lanes], sem.at[h]))
        copies[-1].start()
    for copy in copies:
        copy.wait()


def shifted(value, axis, distance):
    return lax.ppermute(value, axis, [(i, (i + distance) % 4) for i in range(4)])


def cost(flops, bytes_accessed):
    return pl.CostEstimate(flops=flops, bytes_accessed=bytes_accessed, transcendentals=0)


def shards(fields, pre_act, cotangent, weights):
    total = fields.shape[1] * lax.axis_size("y") * lax.axis_size("zl")
    factor = float(total) ** (-0.5)
    vmem = pl.BlockSpec(memory_space=pltpu.VMEM)
    hbm = pl.BlockSpec(memory_space=pltpu.HBM)
    params = pltpu.CompilerParams(vmem_limit_bytes=40 * 2**20)

    def block(*shape):
        return jax.ShapeDtypeStruct(shape, BF16)

    def spectra(steps, after):
        n = len(steps)
        return pl.pallas_call(
            functools.partial(spectra_kernel, steps),
            in_specs=[hbm] * 4,
            out_specs=[vmem] * n,
            out_shape=[block(256, 512)] * n,
            scratch_shapes=[pltpu.VMEM((n, 512, 512), BF16)] * 3
            + [pltpu.VMEM((128, 512), BF16), pltpu.SemaphoreType.DMA((3, n, 2))],
            compiler_params=pltpu.CompilerParams(vmem_limit_bytes=SPECTRA_VMEM),
            cost_estimate=cost(2**28 * n, 2**22 * n),
            name="spectra",
        )(fields, pre_act, cotangent, after)

    (two,) = spectra((2,), fields)
    one, three = spectra((1, 3), two)
    (own,) = spectra((0,), one)
    one, two, three = shifted(one, "y", 1), shifted(two, "y", 2), shifted(three, "y", 3)
    send = pl.pallas_call(
        sum_y_kernel,
        in_specs=[hbm] + [vmem] * 3,
        out_specs=vmem,
        out_shape=block(64, 8, 256),
        scratch_shapes=[pltpu.VMEM((256, 512), BF16), pltpu.SemaphoreType.DMA],
        compiler_params=params,
        name="sum_y",
    )(own, one, two, three)
    got = lax.all_to_all(send, OTHERS, 0, 0, tiled=True)
    mine = lax.dynamic_index_in_dim(weights, lax.axis_index("zl"), 0, keepdims=False)
    send, *sides = pl.pallas_call(
        functools.partial(modes_kernel, factor),
        in_specs=[vmem, vmem],
        out_specs=[vmem] * 5,
        out_shape=[block(16, 4, 8, 128)] + [block(40, 512)] * 4,
        scratch_shapes=[pltpu.VMEM((4, 8, 512), F32)],
        compiler_params=params,
        name="modes",
    )(got, mine)
    sides = [sides[0]] + [shifted(sides[t], "y", t) for t in range(1, 4)]
    got = lax.all_to_all(send.reshape(64, 8, 128), OTHERS, 0, 0, tiled=True)
    own_weight, *sides = pl.pallas_call(
        weight_kernel,
        in_specs=[vmem] * 4,
        out_specs=[vmem] * 4,
        out_shape=[jax.ShapeDtypeStruct((2, 32, 512), F32)] + [block(64, 512)] * 3,
        scratch_shapes=[pltpu.VMEM((2, 4, 32, 512), F32)],
        compiler_params=params,
        cost_estimate=cost(2**26, 2**20),
        name="weight",
    )(*sides)
    sides = [shifted(sides[t - 1], "zl", t) for t in range(1, 4)]
    scratch = [pltpu.VMEM((512, 128), F32), pltpu.VMEM((2, 512, 256), BF16)]
    scratch = scratch + [pltpu.SemaphoreType.DMA((2,))]
    received = {t: shifted(got, "y", t) for t in (2, 1, 3)}
    field_grad, table = pl.pallas_call(
        functools.partial(field_kernel, factor, 0),
        in_specs=[vmem],
        out_specs=[hbm, vmem],
        out_shape=[block(4, 512, 512), block(512, 128)],
        scratch_shapes=scratch,
        compiler_params=params,
        cost_estimate=cost(2**27, 2**20),
        name="field",
    )(got)
    weight_grad = pl.pallas_call(
        place_kernel,
        in_specs=[hbm] + [vmem] * 4,
        out_specs=vmem,
        out_shape=jax.ShapeDtypeStruct((4, 2, 32, 512), F32),
        compiler_params=params,
        cost_estimate=cost(2**20, 2**20),
        name="place",
    )(table, own_weight, *sides)
    for t in (1, 3, 2):
        field_grad = pl.pallas_call(
            functools.partial(field_kernel, factor, t),
            in_specs=[vmem, vmem, hbm],
            out_specs=hbm,
            out_shape=block(4, 512, 512),
            scratch_shapes=scratch,
            input_output_aliases={2: 0},
            compiler_params=params,
            cost_estimate=cost(2**27, 2**20),
            name="field",
        )(received[t], table, field_grad)
    return field_grad, jnp.swapaxes(weight_grad, 2, 3)


def solution(mesh):
    grid = Mesh(mesh.devices.reshape(4, 4, 4, 4), ("y", "zl", "x", "w"))
    space, mode = ("y", "zl"), ("x", "w")
    whole = P(mode, space, None)
    return jax.shard_map(
        shards,
        mesh=grid,
        in_specs=(whole, whole, whole, P(mode, None, None, None)),
        out_specs=(whole, P(mode, None, None, space)),
        check_vma=False,
    )
```

```python
import functools
import math

import jax
import jax.numpy as jnp
from jax import lax
from jax.experimental import pallas as pl
from jax.experimental.pallas import tpu as pltpu
from jax.sharding import Mesh
from jax.sharding import PartitionSpec as P

F32, BF16 = jnp.float32, jnp.bfloat16
OTHERS = ("x", "w", "zl")
SPECTRA_VMEM = 60 * 2**20
NT = (((1,), (1,)), ((), ()))
TN = (((0,), (0,)), ((), ()))


def table_of(points, rows_are_points, offset):
    shape = (points, 128) if rows_are_points else (128, points)
    point = lax.broadcasted_iota(jnp.int32, shape, 0 if rows_are_points else 1) + offset
    row = lax.broadcasted_iota(jnp.int32, shape, 1 if rows_are_points else 0)
    phase = ((row & 63) * point + ((row >> 6) << 11)) & 8191
    quadrant = (phase + 1024) >> 11
    angle = (phase - (quadrant << 11)).astype(F32) * (2.0 * math.pi / 8192.0)
    square = angle * angle
    sine = 1.0 / 362880.0
    for c in (-1.0 / 5040.0, 1.0 / 120.0, -1.0 / 6.0, 1.0):
        sine = sine * square + c
    sine = sine * angle
    cosine = -1.0 / 3628800.0
    for c in (1.0 / 40320.0, -1.0 / 720.0, 1.0 / 24.0, -0.5, 1.0):
        cosine = cosine * square + c
    value = jnp.where((quadrant & 1) == 0, cosine, sine)
    negative = ((quadrant + 1) & 2) != 0
    return jnp.where(negative, -value, value).astype(BF16)


def gelu_slope(values):
    normal_cdf = 0.5 * (1.0 + lax.erf(values * (1.0 / math.sqrt(2.0))))
    density = jnp.exp(-0.5 * values * values) * (1.0 / math.sqrt(2.0 * math.pi))
    return normal_cdf + values * density


def dot(a, b, dims=None):
    if dims is None:
        return jnp.dot(a, b, preferred_element_type=F32)
    return lax.dot_general(a, b, dims, preferred_element_type=F32)


def row_moves(shape, digits, only=(), base=0):
    row = lax.broadcasted_iota(jnp.int32, shape, 0)
    col = lax.broadcasted_iota(jnp.int32, shape, 1)
    source = jnp.full(shape, base, jnp.int32)
    for out_stride, size, in_stride in digits:
        digit = (row >> (out_stride.bit_length() - 1)) & (size - 1)
        source = source + (digit << (in_stride.bit_length() - 1))
    for out_stride, size, wanted in only:
        digit = (row >> (out_stride.bit_length() - 1)) & (size - 1)
        source = jnp.where(digit == wanted, source, -1)
    return jnp.where(source == col, 1.0, 0.0).astype(BF16)


def turned(n):
    row = lax.broadcasted_iota(jnp.int32, (n, n), 0)
    col = lax.broadcasted_iota(jnp.int32, (n, n), 1)
    sign = jnp.where((row & 4) == 0, 1.0, -1.0)
    return jnp.where((row ^ 4) == col, sign, 0.0).astype(BF16)


def spectra_kernel(steps, fields_hbm, pre_hbm, cot_hbm, _, *rest):
    n = len(steps)
    out_hbms, out_refs, (fields, pre, cot, table, sems, out_sems) = rest[:n], rest[n : 2 * n], rest[2 * n :]
    y = lax.axis_index("y")

    def copies(i, h):
        b = (y + steps[i]) & 3
        at = slice(256 * h, 256 * h + 256)
        return [
            pltpu.make_async_copy(hbm.at[b, :, at], vmem.at[i, :, at], sems.at[j, i, h])
            for j, (hbm, vmem) in enumerate(((pre_hbm, pre), (cot_hbm, cot), (fields_hbm, fields)))
        ]

    for i in range(n):
        for h in range(2):
            for copy in copies(i, h):
                copy.start()
    points = table.shape[1]
    table[...] = table_of(points, False, (y * 4 + lax.axis_index("zl")) * points)
    sent = []
    for i in range(n):
        for h in range(2):
            for copy in copies(i, h):
                copy.wait()
            lanes = slice(256 * h, 256 * h + 256)
            slopes = cot[i, :, lanes].astype(F32) * gelu_slope(pre[i, :, lanes].astype(F32))
            out_refs[i][0:128, lanes] = dot(table[...], slopes.astype(BF16)).astype(BF16)
            out_refs[i][128:256, lanes] = dot(table[...], fields[i, :, lanes]).astype(BF16)
            source, target = out_refs[i].at[:, lanes], out_hbms[i].at[:, lanes]
            sent.append(pltpu.make_async_copy(source, target, out_sems.at[i, h]))
            sent[-1].start()
    for copy in sent:
        copy.wait()


def sum_y_kernel(own_hbm, one_ref, two_ref, three_ref, out_ref, own, sem):
    copy = pltpu.make_async_copy(own_hbm, own, sem)
    copy.start()
    total = one_ref[...].astype(F32) + two_ref[...].astype(F32) + three_ref[...].astype(F32)
    copy.wait()
    low = (total + own[...].astype(F32)).astype(BF16)
    out = None
    for h in range(2):
        moves = row_moves((512, 256), [(8, 64, 1), (2, 2, 128), (1, 2, 64)], [(4, 2, h)])
        part = dot(moves, low[:, 256 * h : 256 * h + 256])
        out = part if out is None else out + part
    out_ref[...] = out.reshape(64, 8, 256).astype(BF16)


def modes_kernel(factor, in_ref, w_ref, out_ref, *rest):
    side_refs, chunks = rest[:4], rest[4]
    x, w_mine, zl_mine, y_mine = (lax.axis_index(name) for name in ("x", "w", "zl", "y"))
    total = jnp.sum(in_ref[...].astype(F32).reshape(16, 4, 8, 256), axis=1).reshape(128, 256)
    first_mode = (x == 0) & (w_mine == 0) & (zl_mine == 0)
    is_u = (lax.broadcasted_iota(jnp.int32, (128, 256), 0) & 2) != 0
    g_scale = jnp.where(first_mode, factor, 2.0 * factor)
    low = (total * jnp.where(is_u, factor, g_scale)).astype(BF16)
    digits = [(32, 2, 2), (8, 4, 8), (4, 2, 1), (1, 4, 32)]
    both = [dot(row_moves((64, 128), digits, base=4 * h), low) for h in range(2)]
    both = jnp.concatenate(both, axis=1)
    g, u = both[:32], both[32:]
    g_low = g.astype(BF16)
    g_turned = dot(turned(32), g_low).astype(BF16)
    grad = (dot(g_low, w_ref[0], NT) + dot(g_turned, w_ref[1], NT)).astype(BF16)
    out = None
    for q in range(4):
        moves = row_moves((128, 32), [(32, 4, 1), (8, 4, 8), (1, 2, 4)], [(2, 4, q)])
        part = dot(moves, grad[:, 128 * q : 128 * q + 128])
        out = part if out is None else out + part
    out = out.reshape(16, 8, 128).astype(BF16)
    for zl in range(4):
        out_ref[:, zl] = out
    for y in range(4):
        lanes = slice(128 * y, 128 * y + 128)
        chunks[y] = jnp.concatenate([g[8 * w : 8 * w + 8, lanes] for w in range(4)], axis=1)
    for t in range(4):
        chunk = chunks[(y_mine + t) & 3]
        side_refs[t][...] = jnp.concatenate([u, chunk], axis=0).astype(BF16)


def weight_kernel(*refs):
    in_refs, own_ref, send_refs, result = refs[:4], refs[4], refs[5:8], refs[8]
    u = jnp.concatenate([ref[0:32, :] for ref in in_refs], axis=0)
    g = jnp.concatenate(
        [ref[32:40, 128 * w : 128 * w + 128].astype(F32) for ref in in_refs for w in range(4)],
        axis=0,
    ).astype(BF16)
    both = jnp.concatenate([g, dot(turned(128), g).astype(BF16)], axis=1)
    result[...] = dot(both, u, TN).reshape(2, 4, 32, 512)
    zl_mine = lax.axis_index("zl")
    own_ref[...] = result[:, zl_mine]
    for t in range(1, 4):
        send_refs[t - 1][...] = result[:, (zl_mine + t) & 3].reshape(64, 512).astype(BF16)


def transform(factor, step, in_ref, table_ref, rows, out, field_hbm, sem):
    rows[...] = in_ref[...].astype(F32).reshape(512, 128)
    b = (lax.axis_index("y") - step) & 3
    copies = []
    for h in range(2):
        modes = [
            jnp.concatenate([rows[pl.ds(2 * q + p, 64, stride=8), :] for p in range(2)], axis=0)
            for q in (2 * h, 2 * h + 1)
        ]
        modes = jnp.concatenate(modes, axis=1).astype(BF16)
        out[h] = (dot(table_ref[...], modes) * factor).astype(BF16)
        lanes = slice(256 * h, 256 * h + 256)
        copies.append(pltpu.make_async_copy(out.at[h], field_hbm.at[b, :, lanes], sem.at[h]))
        copies[-1].start()
    return copies


def own_field_kernel(factor, in_ref, field_hbm, table_ref, rows, out, sem):
    points = table_ref.shape[0]
    offset = (lax.axis_index("y") * 4 + lax.axis_index("zl")) * points
    table_ref[...] = table_of(points, True, offset)
    for copy in transform(factor, 0, in_ref, table_ref, rows, out, field_hbm, sem):
        copy.wait()


def last_kernel(factor, *refs):
    in_refs, table_ref, own_ref, weight_in = refs[:3], refs[3], refs[4], refs[5:8]
    field_hbm, weight_hbm, rows, out, weights, sem, weight_sem = refs[9:]
    zl_mine = lax.axis_index("zl")
    copies = [pltpu.make_async_copy(own_ref, weight_hbm.at[zl_mine], weight_sem.at[0])]
    copies[0].start()
    for t in range(1, 4):
        weights[t - 1] = weight_in[t - 1][...].astype(F32).reshape(2, 32, 512)
        target = weight_hbm.at[(zl_mine - t) & 3]
        copies.append(pltpu.make_async_copy(weights.at[t - 1], target, weight_sem.at[t]))
        copies[-1].start()
    for i, t in enumerate((1, 3, 2)):
        copies += transform(factor, t, in_refs[i], table_ref, rows.at[i], out.at[i], field_hbm, sem.at[i])
    for copy in copies:
        copy.wait()


def shifted(value, axis, distance):
    return lax.ppermute(value, axis, [(i, (i + distance) % 4) for i in range(4)])


def cost(flops, bytes_accessed):
    return pl.CostEstimate(flops=flops, bytes_accessed=bytes_accessed, transcendentals=0)


def shards(fields, pre_act, cotangent, weights):
    total = fields.shape[1] * lax.axis_size("y") * lax.axis_size("zl")
    factor = float(total) ** (-0.5)
    vmem = pl.BlockSpec(memory_space=pltpu.VMEM)
    hbm = pl.BlockSpec(memory_space=pltpu.HBM)
    params = pltpu.CompilerParams(vmem_limit_bytes=40 * 2**20)

    def block(*shape):
        return jax.ShapeDtypeStruct(shape, BF16)

    def spectra(steps, after):
        n = len(steps)
        return pl.pallas_call(
            functools.partial(spectra_kernel, steps),
            in_specs=[hbm] * 4,
            out_specs=[hbm] * n,
            out_shape=[block(256, 512)] * n,
            scratch_shapes=[pltpu.VMEM((256, 512), BF16)] * n
            + [pltpu.VMEM((n, 512, 512), BF16)] * 3
            + [pltpu.VMEM((128, 512), BF16), pltpu.SemaphoreType.DMA((3, n, 2))]
            + [pltpu.SemaphoreType.DMA((n, 2))],
            compiler_params=pltpu.CompilerParams(vmem_limit_bytes=SPECTRA_VMEM),
            cost_estimate=cost(2**28 * n, 2**22 * n),
            name="spectra",
        )(fields, pre_act, cotangent, after)

    (two,) = spectra((2,), fields)
    one, three = spectra((1, 3), two)
    (own,) = spectra((0,), one)
    one, two, three = shifted(one, "y", 1), shifted(two, "y", 2), shifted(three, "y", 3)
    send = pl.pallas_call(
        sum_y_kernel,
        in_specs=[hbm] + [vmem] * 3,
        out_specs=vmem,
        out_shape=block(64, 8, 256),
        scratch_shapes=[pltpu.VMEM((256, 512), BF16), pltpu.SemaphoreType.DMA],
        compiler_params=params,
        name="sum_y",
    )(own, one, two, three)
    got = lax.all_to_all(send, OTHERS, 0, 0, tiled=True)
    mine = lax.dynamic_index_in_dim(weights, lax.axis_index("zl"), 0, keepdims=False)
    send, *sides = pl.pallas_call(
        functools.partial(modes_kernel, factor),
        in_specs=[vmem, vmem],
        out_specs=[vmem] * 5,
        out_shape=[block(16, 4, 8, 128)] + [block(40, 512)] * 4,
        scratch_shapes=[pltpu.VMEM((4, 8, 512), F32)],
        compiler_params=params,
        name="modes",
    )(got, mine)
    sides = [sides[0]] + [shifted(sides[t], "y", t) for t in range(1, 4)]
    got = lax.all_to_all(send.reshape(64, 8, 128), OTHERS, 0, 0, tiled=True)
    own_weight, *sides = pl.pallas_call(
        weight_kernel,
        in_specs=[vmem] * 4,
        out_specs=[vmem] * 4,
        out_shape=[jax.ShapeDtypeStruct((2, 32, 512), F32)] + [block(64, 512)] * 3,
        scratch_shapes=[pltpu.VMEM((2, 4, 32, 512), F32)],
        compiler_params=params,
        cost_estimate=cost(2**26, 2**20),
        name="weight",
    )(*sides)
    sides = [shifted(sides[t - 1], "zl", t) for t in range(1, 4)]
    received = [shifted(got, "y", t) for t in (1, 3, 2)]
    field_grad, table = pl.pallas_call(
        functools.partial(own_field_kernel, factor),
        in_specs=[vmem],
        out_specs=[hbm, vmem],
        out_shape=[block(4, 512, 512), block(512, 128)],
        scratch_shapes=[
            pltpu.VMEM((512, 128), F32),
            pltpu.VMEM((2, 512, 256), BF16),
            pltpu.SemaphoreType.DMA((2,)),
        ],
        compiler_params=params,
        cost_estimate=cost(2**27, 2**20),
        name="own_field",
    )(got)
    field_grad, weight_grad = pl.pallas_call(
        functools.partial(last_kernel, factor),
        in_specs=[vmem] * 8 + [hbm],
        out_specs=[hbm, hbm],
        out_shape=[block(4, 512, 512), jax.ShapeDtypeStruct((4, 2, 32, 512), F32)],
        scratch_shapes=[
            pltpu.VMEM((3, 512, 128), F32),
            pltpu.VMEM((3, 2, 512, 256), BF16),
            pltpu.VMEM((3, 2, 32, 512), F32),
            pltpu.SemaphoreType.DMA((3, 2)),
            pltpu.SemaphoreType.DMA((4,)),
        ],
        input_output_aliases={8: 0},
        compiler_params=params,
        name="last",
    )(*received, table, own_weight, *sides, field_grad)
    return field_grad, jnp.swapaxes(weight_grad, 2, 3)


def solution(mesh):
    grid = Mesh(mesh.devices.reshape(4, 4, 4, 4), ("y", "zl", "x", "w"))
    space, mode = ("y", "zl"), ("x", "w")
    whole = P(mode, space, None)
    return jax.shard_map(
        shards,
        mesh=grid,
        in_specs=(whole, whole, whole, P(mode, None, None, None)),
        out_specs=(whole, P(mode, None, None, space)),
        check_vma=False,
    )
```

```python
import functools
import math

import jax
import jax.numpy as jnp
from jax import lax
from jax.experimental import pallas as pl
from jax.experimental.pallas import tpu as pltpu
from jax.sharding import Mesh
from jax.sharding import PartitionSpec as P

F32, BF16 = jnp.float32, jnp.bfloat16
OTHERS = ("x", "w", "zl")
NT = (((1,), (1,)), ((), ()))
TN = (((0,), (0,)), ((), ()))


def table_of(points, rows_are_points, offset):
    shape = (points, 128) if rows_are_points else (128, points)
    point = lax.broadcasted_iota(jnp.int32, shape, 0 if rows_are_points else 1) + offset
    row = lax.broadcasted_iota(jnp.int32, shape, 1 if rows_are_points else 0)
    phase = ((row & 63) * point + ((row >> 6) << 11)) & 8191
    quadrant = (phase + 1024) >> 11
    angle = (phase - (quadrant << 11)).astype(F32) * (2.0 * math.pi / 8192.0)
    square = angle * angle
    sine = 1.0 / 362880.0
    for c in (-1.0 / 5040.0, 1.0 / 120.0, -1.0 / 6.0, 1.0):
        sine = sine * square + c
    sine = sine * angle
    cosine = -1.0 / 3628800.0
    for c in (1.0 / 40320.0, -1.0 / 720.0, 1.0 / 24.0, -0.5, 1.0):
        cosine = cosine * square + c
    value = jnp.where((quadrant & 1) == 0, cosine, sine)
    negative = ((quadrant + 1) & 2) != 0
    return jnp.where(negative, -value, value).astype(BF16)


def gelu_slope(values):
    size = jnp.abs(values)
    t = 1.0 / (1.0 + 0.28 * size)
    m = -0.10580839289759565
    for c in (
        0.38987462028162295,
        -0.23699444704250228,
        0.26891093471374405,
        0.06749644895015629,
        0.11652082672551742,
    ):
        m = m * t + c
    below = jnp.exp(-0.5 * values * values) * (m * t - size * (1.0 / math.sqrt(2.0 * math.pi)))
    return jnp.where(values >= 0.0, 1.0 - below, below)


def dot(a, b, dims=None):
    if dims is None:
        return jnp.dot(a, b, preferred_element_type=F32)
    return lax.dot_general(a, b, dims, preferred_element_type=F32)


def row_moves(shape, digits, only=(), base=0):
    row = lax.broadcasted_iota(jnp.int32, shape, 0)
    col = lax.broadcasted_iota(jnp.int32, shape, 1)
    source = jnp.full(shape, base, jnp.int32)
    for out_stride, size, in_stride in digits:
        digit = (row >> (out_stride.bit_length() - 1)) & (size - 1)
        source = source + (digit << (in_stride.bit_length() - 1))
    for out_stride, size, wanted in only:
        digit = (row >> (out_stride.bit_length() - 1)) & (size - 1)
        source = jnp.where(digit == wanted, source, -1)
    return jnp.where(source == col, 1.0, 0.0).astype(BF16)


def turned(n):
    row = lax.broadcasted_iota(jnp.int32, (n, n), 0)
    col = lax.broadcasted_iota(jnp.int32, (n, n), 1)
    sign = jnp.where((row & 4) == 0, 1.0, -1.0)
    return jnp.where((row ^ 4) == col, sign, 0.0).astype(BF16)


def spectra_kernel(steps, fields_hbm, pre_hbm, cot_hbm, _, *rest):
    n = len(steps)
    token_ref, *rest = rest
    token_ref[...] = jnp.zeros_like(token_ref)
    out_hbms, rest = rest[:n], rest[n:]
    if steps == (0,):
        moves_ref, *rest = rest
    out_refs, (fields, pre, cot, table, sems, out_sems) = rest[:n], rest[n:]
    y = lax.axis_index("y")

    def copies(i, h):
        b = (y + steps[i]) & 3
        at = slice(256 * h, 256 * h + 256)
        return [
            pltpu.make_async_copy(hbm.at[b, :, at], vmem.at[i, :, at], sems.at[j, i, h])
            for j, (hbm, vmem) in enumerate(((pre_hbm, pre), (cot_hbm, cot), (fields_hbm, fields)))
        ]

    for i in range(n):
        for h in range(2):
            for copy in copies(i, h):
                copy.start()
    points = table.shape[1]
    table[...] = table_of(points, False, (y * 4 + lax.axis_index("zl")) * points)
    if steps == (0,):
        for h in range(2):
            digits = [(8, 64, 1), (2, 2, 128), (1, 2, 64)]
            moves_ref[h] = row_moves((512, 256), digits, [(4, 2, h)])
    sent = []
    for i in range(n):
        for h in range(2):
            for copy in copies(i, h):
                copy.wait()
            lanes = slice(256 * h, 256 * h + 256)
            slopes = cot[i, :, lanes].astype(F32) * gelu_slope(pre[i, :, lanes].astype(F32))
            out_refs[i][0:128, lanes] = dot(table[...], slopes.astype(BF16)).astype(BF16)
            out_refs[i][128:256, lanes] = dot(table[...], fields[i, :, lanes]).astype(BF16)
            source, target = out_refs[i].at[:, lanes], out_hbms[i].at[:, lanes]
            sent.append(pltpu.make_async_copy(source, target, out_sems.at[i, h]))
            sent[-1].start()
    for copy in sent:
        copy.wait()


def sum_y_kernel(moves_ref, own_ref, one_ref, two_ref, three_ref, out_ref):
    total = one_ref[...].astype(F32) + two_ref[...].astype(F32) + three_ref[...].astype(F32)
    low = (total + own_ref[...].astype(F32)).astype(BF16)
    out = dot(moves_ref[0], low[:, :256]) + dot(moves_ref[1], low[:, 256:])
    out_ref[...] = out.reshape(64, 8, 256).astype(BF16)


def modes_kernel(factor, in_ref, w_ref, out_ref, *rest):
    side_refs, chunks = rest[:4], rest[4]
    x, w_mine, zl_mine, y_mine = (lax.axis_index(name) for name in ("x", "w", "zl", "y"))
    total = jnp.sum(in_ref[...].astype(F32).reshape(16, 4, 8, 256), axis=1).reshape(128, 256)
    first_mode = (x == 0) & (w_mine == 0) & (zl_mine == 0)
    is_u = (lax.broadcasted_iota(jnp.int32, (128, 256), 0) & 2) != 0
    g_scale = jnp.where(first_mode, factor, 2.0 * factor)
    low = (total * jnp.where(is_u, factor, g_scale)).astype(BF16)
    digits = [(32, 2, 2), (8, 4, 8), (4, 2, 1), (1, 4, 32)]
    both = [dot(row_moves((64, 128), digits, base=4 * h), low) for h in range(2)]
    both = jnp.concatenate(both, axis=1)
    g, u = both[:32], both[32:]
    g_low = g.astype(BF16)
    g_turned = dot(turned(32), g_low).astype(BF16)
    grad = (dot(g_low, w_ref[0], NT) + dot(g_turned, w_ref[1], NT)).astype(BF16)
    out = None
    for q in range(4):
        moves = row_moves((128, 32), [(32, 4, 1), (8, 4, 8), (1, 2, 4)], [(2, 4, q)])
        part = dot(moves, grad[:, 128 * q : 128 * q + 128])
        out = part if out is None else out + part
    out = out.reshape(16, 8, 128).astype(BF16)
    for zl in range(4):
        out_ref[:, zl] = out
    for y in range(4):
        lanes = slice(128 * y, 128 * y + 128)
        chunks[y] = jnp.concatenate([g[8 * w : 8 * w + 8, lanes] for w in range(4)], axis=1)
    for t in range(4):
        chunk = chunks[(y_mine + t) & 3]
        side_refs[t][...] = jnp.concatenate([u, chunk], axis=0).astype(BF16)


def weight_kernel(*refs):
    in_refs, own_ref, send_refs, result = refs[:4], refs[4], refs[5:8], refs[8]
    u = jnp.concatenate([ref[0:32, :] for ref in in_refs], axis=0)
    g = jnp.concatenate(
        [ref[32:40, 128 * w : 128 * w + 128].astype(F32) for ref in in_refs for w in range(4)],
        axis=0,
    ).astype(BF16)
    both = jnp.concatenate([g, dot(turned(128), g).astype(BF16)], axis=1)
    result[...] = dot(both, u, TN).reshape(2, 4, 32, 512)
    zl_mine = lax.axis_index("zl")
    own_ref[...] = result[:, zl_mine]
    for t in range(1, 4):
        send_refs[t - 1][...] = result[:, (zl_mine + t) & 3].reshape(64, 512).astype(BF16)


def transform(factor, step, in_ref, table_ref, rows, out, field_hbm, sem):
    rows[...] = in_ref[...].astype(F32).reshape(512, 128)
    b = (lax.axis_index("y") - step) & 3
    copies = []
    for h in range(2):
        modes = [
            jnp.concatenate([rows[pl.ds(2 * q + p, 64, stride=8), :] for p in range(2)], axis=0)
            for q in (2 * h, 2 * h + 1)
        ]
        modes = jnp.concatenate(modes, axis=1).astype(BF16)
        out[h] = (dot(table_ref[...], modes) * factor).astype(BF16)
        lanes = slice(256 * h, 256 * h + 256)
        copies.append(pltpu.make_async_copy(out.at[h], field_hbm.at[b, :, lanes], sem.at[h]))
        copies[-1].start()
    return copies


def own_field_kernel(factor, in_ref, field_hbm, table_ref, rows, out, sem):
    points = table_ref.shape[0]
    offset = (lax.axis_index("y") * 4 + lax.axis_index("zl")) * points
    table_ref[...] = table_of(points, True, offset)
    for copy in transform(factor, 0, in_ref, table_ref, rows, out, field_hbm, sem):
        copy.wait()


def last_kernel(factor, *refs):
    in_refs, table_ref, own_ref, weight_in = refs[:3], refs[3], refs[4], refs[5:8]
    field_hbm, weight_hbm, rows, out, weights, sem, weight_sem = refs[9:]
    zl_mine = lax.axis_index("zl")
    copies = [pltpu.make_async_copy(own_ref, weight_hbm.at[zl_mine], weight_sem.at[0])]
    copies[0].start()
    for t in range(1, 4):
        weights[t - 1] = weight_in[t - 1][...].astype(F32).reshape(2, 32, 512)
        target = weight_hbm.at[(zl_mine - t) & 3]
        copies.append(pltpu.make_async_copy(weights.at[t - 1], target, weight_sem.at[t]))
        copies[-1].start()
    for i, t in enumerate((1, 3, 2)):
        copies += transform(factor, t, in_refs[i], table_ref, rows.at[i], out.at[i], field_hbm, sem.at[i])
    for copy in copies:
        copy.wait()


def shifted(value, axis, distance):
    return lax.ppermute(value, axis, [(i, (i + distance) % 4) for i in range(4)])


def cost(flops, bytes_accessed):
    return pl.CostEstimate(flops=flops, bytes_accessed=bytes_accessed, transcendentals=0)


def shards(fields, pre_act, cotangent, weights):
    total = fields.shape[1] * lax.axis_size("y") * lax.axis_size("zl")
    factor = float(total) ** (-0.5)
    vmem = pl.BlockSpec(memory_space=pltpu.VMEM)
    hbm = pl.BlockSpec(memory_space=pltpu.HBM)
    params = pltpu.CompilerParams(vmem_limit_bytes=40 * 2**20)

    def block(*shape):
        return jax.ShapeDtypeStruct(shape, BF16)

    def spectra(steps, after):
        n = len(steps)
        moves = [block(2, 512, 256)] if steps == (0,) else []
        return pl.pallas_call(
            functools.partial(spectra_kernel, steps),
            in_specs=[hbm] * 4,
            out_specs=[vmem] + [hbm] * n + [vmem] * len(moves),
            out_shape=[jax.ShapeDtypeStruct((8, 128), F32)] + [block(256, 512)] * n + moves,
            scratch_shapes=[pltpu.VMEM((256, 512), BF16)] * n
            + [pltpu.VMEM((n, 512, 512), BF16)] * 3
            + [pltpu.VMEM((128, 512), BF16), pltpu.SemaphoreType.DMA((3, n, 2))]
            + [pltpu.SemaphoreType.DMA((n, 2))],
            compiler_params=pltpu.CompilerParams(vmem_limit_bytes=52 * 2**20),
            cost_estimate=cost(2**28 * n, 2**22 * n),
            name="spectra",
        )(fields, pre_act, cotangent, after)

    token, two = spectra((2,), fields)
    token, one, three = spectra((1, 3), token)
    _, own, moves = spectra((0,), token)
    one, two, three = shifted(one, "y", 1), shifted(two, "y", 2), shifted(three, "y", 3)
    send = pl.pallas_call(
        sum_y_kernel,
        in_specs=[vmem] * 5,
        out_specs=vmem,
        out_shape=block(64, 8, 256),
        compiler_params=params,
        name="sum_y",
    )(moves, own, one, two, three)
    got = lax.all_to_all(send, OTHERS, 0, 0, tiled=True)
    mine = lax.dynamic_index_in_dim(weights, lax.axis_index("zl"), 0, keepdims=False)
    send, *sides = pl.pallas_call(
        functools.partial(modes_kernel, factor),
        in_specs=[vmem, vmem],
        out_specs=[vmem] * 5,
        out_shape=[block(16, 4, 8, 128)] + [block(40, 512)] * 4,
        scratch_shapes=[pltpu.VMEM((4, 8, 512), F32)],
        compiler_params=params,
        name="modes",
    )(got, mine)
    sides = [sides[0]] + [shifted(sides[t], "y", t) for t in range(1, 4)]
    got = lax.all_to_all(send.reshape(64, 8, 128), OTHERS, 0, 0, tiled=True)
    own_weight, *sides = pl.pallas_call(
        weight_kernel,
        in_specs=[vmem] * 4,
        out_specs=[vmem] * 4,
        out_shape=[jax.ShapeDtypeStruct((2, 32, 512), F32)] + [block(64, 512)] * 3,
        scratch_shapes=[pltpu.VMEM((2, 4, 32, 512), F32)],
        compiler_params=params,
        cost_estimate=cost(2**26, 2**20),
        name="weight",
    )(*sides)
    sides = [shifted(sides[t - 1], "zl", t) for t in range(1, 4)]
    received = [shifted(got, "y", t) for t in (1, 3, 2)]
    field_grad, table = pl.pallas_call(
        functools.partial(own_field_kernel, factor),
        in_specs=[vmem],
        out_specs=[hbm, vmem],
        out_shape=[block(4, 512, 512), block(512, 128)],
        scratch_shapes=[
            pltpu.VMEM((512, 128), F32),
            pltpu.VMEM((2, 512, 256), BF16),
            pltpu.SemaphoreType.DMA((2,)),
        ],
        compiler_params=params,
        cost_estimate=cost(2**27, 2**20),
        name="own_field",
    )(got)
    field_grad, weight_grad = pl.pallas_call(
        functools.partial(last_kernel, factor),
        in_specs=[vmem] * 8 + [hbm],
        out_specs=[hbm, hbm],
        out_shape=[block(4, 512, 512), jax.ShapeDtypeStruct((4, 2, 32, 512), F32)],
        scratch_shapes=[
            pltpu.VMEM((3, 512, 128), F32),
            pltpu.VMEM((3, 2, 512, 256), BF16),
            pltpu.VMEM((3, 2, 32, 512), F32),
            pltpu.SemaphoreType.DMA((3, 2)),
            pltpu.SemaphoreType.DMA((4,)),
        ],
        input_output_aliases={8: 0},
        compiler_params=params,
        name="last",
    )(*received, table, own_weight, *sides, field_grad)
    return field_grad, jnp.swapaxes(weight_grad, 2, 3)


def solution(mesh):
    grid = Mesh(mesh.devices.reshape(4, 4, 4, 4), ("y", "zl", "x", "w"))
    space, mode = ("y", "zl"), ("x", "w")
    whole = P(mode, space, None)
    return jax.shard_map(
        shards,
        mesh=grid,
        in_specs=(whole, whole, whole, P(mode, None, None, None)),
        out_specs=(whole, P(mode, None, None, space)),
        check_vma=False,
    )
```

```python
import functools
import math

import jax
import jax.numpy as jnp
from jax import lax
from jax.experimental import pallas as pl
from jax.experimental.pallas import tpu as pltpu
from jax.sharding import Mesh
from jax.sharding import PartitionSpec as P

F32, BF16 = jnp.float32, jnp.bfloat16
OTHERS = ("x", "w", "zl")
NT = (((1,), (1,)), ((), ()))
TN = (((0,), (0,)), ((), ()))


def table_of(points, rows_are_points, offset):
    shape = (points, 128) if rows_are_points else (128, points)
    point = lax.broadcasted_iota(jnp.int32, shape, 0 if rows_are_points else 1) + offset
    row = lax.broadcasted_iota(jnp.int32, shape, 1 if rows_are_points else 0)
    phase = ((row & 63) * point + ((row >> 6) << 11)) & 8191
    quadrant = (phase + 1024) >> 11
    angle = (phase - (quadrant << 11)).astype(F32) * (2.0 * math.pi / 8192.0)
    square = angle * angle
    sine = 1.0 / 362880.0
    for c in (-1.0 / 5040.0, 1.0 / 120.0, -1.0 / 6.0, 1.0):
        sine = sine * square + c
    sine = sine * angle
    cosine = -1.0 / 3628800.0
    for c in (1.0 / 40320.0, -1.0 / 720.0, 1.0 / 24.0, -0.5, 1.0):
        cosine = cosine * square + c
    value = jnp.where((quadrant & 1) == 0, cosine, sine)
    negative = ((quadrant + 1) & 2) != 0
    return jnp.where(negative, -value, value).astype(BF16)


def gelu_slope(values):
    normal_cdf = 0.5 * (1.0 + lax.erf(values * (1.0 / math.sqrt(2.0))))
    density = jnp.exp(-0.5 * values * values) * (1.0 / math.sqrt(2.0 * math.pi))
    return normal_cdf + values * density


def dot(a, b, dims=None):
    if dims is None:
        return jnp.dot(a, b, preferred_element_type=F32)
    return lax.dot_general(a, b, dims, preferred_element_type=F32)


def row_moves(shape, digits, only=(), base=0):
    row = lax.broadcasted_iota(jnp.int32, shape, 0)
    col = lax.broadcasted_iota(jnp.int32, shape, 1)
    source = jnp.full(shape, base, jnp.int32)
    for out_stride, size, in_stride in digits:
        digit = (row >> (out_stride.bit_length() - 1)) & (size - 1)
        source = source + (digit << (in_stride.bit_length() - 1))
    for out_stride, size, wanted in only:
        digit = (row >> (out_stride.bit_length() - 1)) & (size - 1)
        source = jnp.where(digit == wanted, source, -1)
    return jnp.where(source == col, 1.0, 0.0).astype(BF16)


def turned(n):
    row = lax.broadcasted_iota(jnp.int32, (n, n), 0)
    col = lax.broadcasted_iota(jnp.int32, (n, n), 1)
    sign = jnp.where((row & 4) == 0, 1.0, -1.0)
    return jnp.where((row ^ 4) == col, sign, 0.0).astype(BF16)


def spectra_kernel(steps, fields_hbm, pre_hbm, cot_hbm, _, *rest):
    n = len(steps)
    token_ref, *rest = rest
    token_ref[...] = jnp.zeros_like(token_ref)
    out_hbms, rest = rest[:n], rest[n:]
    if steps == (0,):
        moves_ref, *rest = rest
    out_refs, (fields, pre, cot, table, sems, out_sems) = rest[:n], rest[n:]
    y = lax.axis_index("y")

    def copies(i, h):
        b = (y + steps[i]) & 3
        at = slice(256 * h, 256 * h + 256)
        return [
            pltpu.make_async_copy(hbm.at[b, :, at], vmem.at[i, :, at], sems.at[j, i, h])
            for j, (hbm, vmem) in enumerate(((pre_hbm, pre), (cot_hbm, cot), (fields_hbm, fields)))
        ]

    for i in range(n):
        for h in range(2):
            for copy in copies(i, h):
                copy.start()
    points = table.shape[1]
    table[...] = table_of(points, False, (y * 4 + lax.axis_index("zl")) * points)
    if steps == (0,):
        for h in range(2):
            digits = [(8, 64, 1), (2, 2, 128), (1, 2, 64)]
            moves_ref[h] = row_moves((512, 256), digits, [(4, 2, h)])
    sent = []
    for i in range(n):
        for h in range(2):
            for copy in copies(i, h):
                copy.wait()
            lanes = slice(256 * h, 256 * h + 256)
            slopes = cot[i, :, lanes].astype(F32) * gelu_slope(pre[i, :, lanes].astype(F32))
            out_refs[i][0:128, lanes] = dot(table[...], slopes.astype(BF16)).astype(BF16)
            out_refs[i][128:256, lanes] = dot(table[...], fields[i, :, lanes]).astype(BF16)
            source, target = out_refs[i].at[:, lanes], out_hbms[i].at[:, lanes]
            sent.append(pltpu.make_async_copy(source, target, out_sems.at[i, h]))
            sent[-1].start()
    for copy in sent:
        copy.wait()


def sum_y_kernel(moves_ref, own_ref, one_ref, two_ref, three_ref, out_hbm, out, sems):
    total = one_ref[...].astype(F32) + two_ref[...].astype(F32) + three_ref[...].astype(F32)
    low = (total + own_ref[...].astype(F32)).astype(BF16)
    copies = []
    for i in range(4):
        rows, blocks = slice(128 * i, 128 * i + 128), slice(16 * i, 16 * i + 16)
        part = dot(moves_ref[0, rows], low[:, :256]) + dot(moves_ref[1, rows], low[:, 256:])
        out[blocks] = part.reshape(16, 8, 256).astype(BF16)
        copies.append(pltpu.make_async_copy(out.at[blocks], out_hbm.at[blocks], sems.at[i]))
        copies[-1].start()
    for copy in copies:
        copy.wait()


def modes_kernel(factor, in_ref, w_ref, out_hbm, *rest):
    side_refs, (chunks, out_ref, sem) = rest[:4], rest[4:]
    x, w_mine, zl_mine, y_mine = (lax.axis_index(name) for name in ("x", "w", "zl", "y"))
    total = jnp.sum(in_ref[...].astype(F32).reshape(16, 4, 8, 256), axis=1).reshape(128, 256)
    first_mode = (x == 0) & (w_mine == 0) & (zl_mine == 0)
    is_u = (lax.broadcasted_iota(jnp.int32, (128, 256), 0) & 2) != 0
    g_scale = jnp.where(first_mode, factor, 2.0 * factor)
    low = (total * jnp.where(is_u, factor, g_scale)).astype(BF16)
    digits = [(32, 2, 2), (8, 4, 8), (4, 2, 1), (1, 4, 32)]
    both = [dot(row_moves((64, 128), digits, base=4 * h), low) for h in range(2)]
    both = jnp.concatenate(both, axis=1)
    g, u = both[:32], both[32:]
    g_low = g.astype(BF16)
    g_turned = dot(turned(32), g_low).astype(BF16)
    grad = (dot(g_low, w_ref[0], NT) + dot(g_turned, w_ref[1], NT)).astype(BF16)
    out = None
    for q in range(4):
        moves = row_moves((128, 32), [(32, 4, 1), (8, 4, 8), (1, 2, 4)], [(2, 4, q)])
        part = dot(moves, grad[:, 128 * q : 128 * q + 128])
        out = part if out is None else out + part
    out = out.reshape(16, 8, 128).astype(BF16)
    for zl in range(4):
        out_ref[:, zl] = out
    copy = pltpu.make_async_copy(out_ref, out_hbm, sem)
    copy.start()
    for y in range(4):
        lanes = slice(128 * y, 128 * y + 128)
        chunks[y] = jnp.concatenate([g[8 * w : 8 * w + 8, lanes] for w in range(4)], axis=1)
    for t in range(4):
        chunk = chunks[(y_mine + t) & 3]
        side_refs[t][...] = jnp.concatenate([u, chunk], axis=0).astype(BF16)
    copy.wait()


def weight_kernel(*refs):
    in_refs, own_ref, send_refs, result = refs[:4], refs[4], refs[5:8], refs[8]
    u = jnp.concatenate([ref[0:32, :] for ref in in_refs], axis=0)
    g = jnp.concatenate(
        [ref[32:40, 128 * w : 128 * w + 128].astype(F32) for ref in in_refs for w in range(4)],
        axis=0,
    ).astype(BF16)
    both = jnp.concatenate([g, dot(turned(128), g).astype(BF16)], axis=1)
    result[...] = dot(both, u, TN).reshape(2, 4, 32, 512)
    zl_mine = lax.axis_index("zl")
    own_ref[...] = result[:, zl_mine]
    for t in range(1, 4):
        send_refs[t - 1][...] = result[:, (zl_mine + t) & 3].reshape(64, 512).astype(BF16)


def transform(factor, step, in_ref, table_ref, rows, out, field_hbm, sem):
    rows[...] = in_ref[...].astype(F32).reshape(512, 128)
    b = (lax.axis_index("y") - step) & 3
    copies = []
    for h in range(2):
        modes = [
            jnp.concatenate([rows[pl.ds(2 * q + p, 64, stride=8), :] for p in range(2)], axis=0)
            for q in (2 * h, 2 * h + 1)
        ]
        modes = jnp.concatenate(modes, axis=1).astype(BF16)
        out[h] = (dot(table_ref[...], modes) * factor).astype(BF16)
        lanes = slice(256 * h, 256 * h + 256)
        copies.append(pltpu.make_async_copy(out.at[h], field_hbm.at[b, :, lanes], sem.at[h]))
        copies[-1].start()
    return copies


def own_field_kernel(factor, in_ref, field_hbm, table_ref, rows, out, sem):
    points = table_ref.shape[0]
    offset = (lax.axis_index("y") * 4 + lax.axis_index("zl")) * points
    table_ref[...] = table_of(points, True, offset)
    for copy in transform(factor, 0, in_ref, table_ref, rows, out, field_hbm, sem):
        copy.wait()


def last_kernel(factor, *refs):
    in_refs, table_ref, own_ref, weight_in = refs[:3], refs[3], refs[4], refs[5:8]
    field_hbm, weight_hbm, rows, out, weights, sem, weight_sem = refs[9:]
    zl_mine = lax.axis_index("zl")
    copies = [pltpu.make_async_copy(own_ref, weight_hbm.at[zl_mine], weight_sem.at[0])]
    copies[0].start()
    for t in range(1, 4):
        weights[t - 1] = weight_in[t - 1][...].astype(F32).reshape(2, 32, 512)
        target = weight_hbm.at[(zl_mine - t) & 3]
        copies.append(pltpu.make_async_copy(weights.at[t - 1], target, weight_sem.at[t]))
        copies[-1].start()
    for i, t in enumerate((1, 3, 2)):
        copies += transform(factor, t, in_refs[i], table_ref, rows.at[i], out.at[i], field_hbm, sem.at[i])
    for copy in copies:
        copy.wait()


def shifted(value, axis, distance):
    return lax.ppermute(value, axis, [(i, (i + distance) % 4) for i in range(4)])


def cost(flops, bytes_accessed):
    return pl.CostEstimate(flops=flops, bytes_accessed=bytes_accessed, transcendentals=0)


def shards(fields, pre_act, cotangent, weights):
    total = fields.shape[1] * lax.axis_size("y") * lax.axis_size("zl")
    factor = float(total) ** (-0.5)
    vmem = pl.BlockSpec(memory_space=pltpu.VMEM)
    hbm = pl.BlockSpec(memory_space=pltpu.HBM)
    params = pltpu.CompilerParams(vmem_limit_bytes=40 * 2**20)

    def block(*shape):
        return jax.ShapeDtypeStruct(shape, BF16)

    def spectra(steps, after):
        n = len(steps)
        moves = [block(2, 512, 256)] if steps == (0,) else []
        return pl.pallas_call(
            functools.partial(spectra_kernel, steps),
            in_specs=[hbm] * 4,
            out_specs=[vmem] + [hbm] * n + [vmem] * len(moves),
            out_shape=[jax.ShapeDtypeStruct((8, 128), F32)] + [block(256, 512)] * n + moves,
            scratch_shapes=[pltpu.VMEM((256, 512), BF16)] * n
            + [pltpu.VMEM((n, 512, 512), BF16)] * 3
            + [pltpu.VMEM((128, 512), BF16), pltpu.SemaphoreType.DMA((3, n, 2))]
            + [pltpu.SemaphoreType.DMA((n, 2))],
            compiler_params=pltpu.CompilerParams(vmem_limit_bytes=52 * 2**20),
            cost_estimate=cost(2**28 * n, 2**22 * n),
            name="spectra",
        )(fields, pre_act, cotangent, after)

    token, two = spectra((2,), fields)
    token, one, three = spectra((1, 3), token)
    _, own, moves = spectra((0,), token)
    one, two, three = shifted(one, "y", 1), shifted(two, "y", 2), shifted(three, "y", 3)
    send = pl.pallas_call(
        sum_y_kernel,
        in_specs=[vmem] * 5,
        out_specs=hbm,
        out_shape=block(64, 8, 256),
        scratch_shapes=[pltpu.VMEM((64, 8, 256), BF16), pltpu.SemaphoreType.DMA((4,))],
        compiler_params=params,
        name="sum_y",
    )(moves, own, one, two, three)
    got = lax.all_to_all(send, OTHERS, 0, 0, tiled=True)
    mine = lax.dynamic_index_in_dim(weights, lax.axis_index("zl"), 0, keepdims=False)
    send, *sides = pl.pallas_call(
        functools.partial(modes_kernel, factor),
        in_specs=[vmem, vmem],
        out_specs=[hbm] + [vmem] * 4,
        out_shape=[block(16, 4, 8, 128)] + [block(40, 512)] * 4,
        scratch_shapes=[
            pltpu.VMEM((4, 8, 512), F32),
            pltpu.VMEM((16, 4, 8, 128), BF16),
            pltpu.SemaphoreType.DMA,
        ],
        compiler_params=params,
        name="modes",
    )(got, mine)
    sides = [sides[0]] + [shifted(sides[t], "y", t) for t in range(1, 4)]
    got = lax.all_to_all(send.reshape(64, 8, 128), OTHERS, 0, 0, tiled=True)
    own_weight, *sides = pl.pallas_call(
        weight_kernel,
        in_specs=[vmem] * 4,
        out_specs=[vmem] * 4,
        out_shape=[jax.ShapeDtypeStruct((2, 32, 512), F32)] + [block(64, 512)] * 3,
        scratch_shapes=[pltpu.VMEM((2, 4, 32, 512), F32)],
        compiler_params=params,
        cost_estimate=cost(2**26, 2**20),
        name="weight",
    )(*sides)
    sides = [shifted(sides[t - 1], "zl", t) for t in range(1, 4)]
    received = [shifted(got, "y", t) for t in (1, 3, 2)]
    field_grad, table = pl.pallas_call(
        functools.partial(own_field_kernel, factor),
        in_specs=[vmem],
        out_specs=[hbm, vmem],
        out_shape=[block(4, 512, 512), block(512, 128)],
        scratch_shapes=[
            pltpu.VMEM((512, 128), F32),
            pltpu.VMEM((2, 512, 256), BF16),
            pltpu.SemaphoreType.DMA((2,)),
        ],
        compiler_params=params,
        cost_estimate=cost(2**27, 2**20),
        name="own_field",
    )(got)
    field_grad, weight_grad = pl.pallas_call(
        functools.partial(last_kernel, factor),
        in_specs=[vmem] * 8 + [hbm],
        out_specs=[hbm, hbm],
        out_shape=[block(4, 512, 512), jax.ShapeDtypeStruct((4, 2, 32, 512), F32)],
        scratch_shapes=[
            pltpu.VMEM((3, 512, 128), F32),
            pltpu.VMEM((3, 2, 512, 256), BF16),
            pltpu.VMEM((3, 2, 32, 512), F32),
            pltpu.SemaphoreType.DMA((3, 2)),
            pltpu.SemaphoreType.DMA((4,)),
        ],
        input_output_aliases={8: 0},
        compiler_params=params,
        name="last",
    )(*received, table, own_weight, *sides, field_grad)
    return field_grad, jnp.swapaxes(weight_grad, 2, 3)


def solution(mesh):
    grid = Mesh(mesh.devices.reshape(4, 4, 4, 4), ("y", "zl", "x", "w"))
    space, mode = ("y", "zl"), ("x", "w")
    whole = P(mode, space, None)
    return jax.shard_map(
        shards,
        mesh=grid,
        in_specs=(whole, whole, whole, P(mode, None, None, None)),
        out_specs=(whole, P(mode, None, None, space)),
        check_vma=False,
    )
```

```python
import functools
import math

import jax
import jax.numpy as jnp
from jax import lax
from jax.experimental import pallas as pl
from jax.experimental.pallas import tpu as pltpu
from jax.sharding import Mesh
from jax.sharding import PartitionSpec as P

F32, BF16 = jnp.float32, jnp.bfloat16
OTHERS = ("x", "w", "zl")
NT = (((1,), (1,)), ((), ()))
TN = (((0,), (0,)), ((), ()))


def table_of(points, rows_are_points, offset):
    shape = (points, 128) if rows_are_points else (128, points)
    point = lax.broadcasted_iota(jnp.int32, shape, 0 if rows_are_points else 1) + offset
    row = lax.broadcasted_iota(jnp.int32, shape, 1 if rows_are_points else 0)
    phase = ((row & 63) * point + ((row >> 6) << 11)) & 8191
    quadrant = (phase + 1024) >> 11
    angle = (phase - (quadrant << 11)).astype(F32) * (2.0 * math.pi / 8192.0)
    square = angle * angle
    sine = 1.0 / 362880.0
    for c in (-1.0 / 5040.0, 1.0 / 120.0, -1.0 / 6.0, 1.0):
        sine = sine * square + c
    sine = sine * angle
    cosine = -1.0 / 3628800.0
    for c in (1.0 / 40320.0, -1.0 / 720.0, 1.0 / 24.0, -0.5, 1.0):
        cosine = cosine * square + c
    value = jnp.where((quadrant & 1) == 0, cosine, sine)
    negative = ((quadrant + 1) & 2) != 0
    return jnp.where(negative, -value, value).astype(BF16)


def gelu_slope(values):
    normal_cdf = 0.5 * (1.0 + lax.erf(values * (1.0 / math.sqrt(2.0))))
    density = jnp.exp(-0.5 * values * values) * (1.0 / math.sqrt(2.0 * math.pi))
    return normal_cdf + values * density


def dot(a, b, dims=None):
    if dims is None:
        return jnp.dot(a, b, preferred_element_type=F32)
    return lax.dot_general(a, b, dims, preferred_element_type=F32)


def row_moves(shape, digits, only=(), base=0):
    row = lax.broadcasted_iota(jnp.int32, shape, 0)
    col = lax.broadcasted_iota(jnp.int32, shape, 1)
    source = jnp.full(shape, base, jnp.int32)
    for out_stride, size, in_stride in digits:
        digit = (row >> (out_stride.bit_length() - 1)) & (size - 1)
        source = source + (digit << (in_stride.bit_length() - 1))
    for out_stride, size, wanted in only:
        digit = (row >> (out_stride.bit_length() - 1)) & (size - 1)
        source = jnp.where(digit == wanted, source, -1)
    return jnp.where(source == col, 1.0, 0.0).astype(BF16)


def turned(n):
    row = lax.broadcasted_iota(jnp.int32, (n, n), 0)
    col = lax.broadcasted_iota(jnp.int32, (n, n), 1)
    sign = jnp.where((row & 4) == 0, 1.0, -1.0)
    return jnp.where((row ^ 4) == col, sign, 0.0).astype(BF16)


def spectra_kernel(steps, fields_hbm, pre_hbm, cot_hbm, _, *rest):
    n = len(steps)
    token_ref, *rest = rest
    token_ref[...] = jnp.zeros_like(token_ref)
    out_hbms, rest = rest[:n], rest[n:]
    if steps == (0,):
        moves_ref, *rest = rest
    out_refs, (fields, pre, cot, table, sems, out_sems) = rest[:n], rest[n:]
    y = lax.axis_index("y")

    def copies(i, h):
        b = (y + steps[i]) & 3
        at = slice(256 * h, 256 * h + 256)
        return [
            pltpu.make_async_copy(hbm.at[b, :, at], vmem.at[i, :, at], sems.at[j, i, h])
            for j, (hbm, vmem) in enumerate(((pre_hbm, pre), (cot_hbm, cot), (fields_hbm, fields)))
        ]

    for i in range(n):
        for h in range(2):
            for copy in copies(i, h):
                copy.start()
    points = table.shape[1]
    table[...] = table_of(points, False, (y * 4 + lax.axis_index("zl")) * points)
    if steps == (0,):
        for h in range(2):
            digits = [(8, 64, 1), (2, 2, 128), (1, 2, 64)]
            moves_ref[h] = row_moves((512, 256), digits, [(4, 2, h)])
    sent = []
    for i in range(n):
        for h in range(2):
            for copy in copies(i, h):
                copy.wait()
            lanes = slice(256 * h, 256 * h + 256)
            slopes = cot[i, :, lanes].astype(F32) * gelu_slope(pre[i, :, lanes].astype(F32))
            out_refs[i][0:128, lanes] = dot(table[...], slopes.astype(BF16)).astype(BF16)
            out_refs[i][128:256, lanes] = dot(table[...], fields[i, :, lanes]).astype(BF16)
            source, target = out_refs[i].at[:, lanes], out_hbms[i].at[:, lanes]
            sent.append(pltpu.make_async_copy(source, target, out_sems.at[i, h]))
            sent[-1].start()
    for copy in sent:
        copy.wait()


def sum_y_kernel(moves_ref, own_ref, one_ref, two_ref, three_ref, out_hbm, out, sems):
    total = one_ref[...].astype(F32) + two_ref[...].astype(F32) + three_ref[...].astype(F32)
    low = (total + own_ref[...].astype(F32)).astype(BF16)
    copies = []
    for i in range(2):
        rows, blocks = slice(256 * i, 256 * i + 256), slice(32 * i, 32 * i + 32)
        part = dot(moves_ref[0, rows], low[:, :256]) + dot(moves_ref[1, rows], low[:, 256:])
        out[blocks] = part.reshape(32, 8, 256).astype(BF16)
        copies.append(pltpu.make_async_copy(out.at[blocks], out_hbm.at[blocks], sems.at[i]))
        copies[-1].start()
    for copy in copies:
        copy.wait()


def modes_kernel(factor, in_ref, w_ref, out_hbm, *rest):
    side_refs, (chunks, out_ref, sem) = rest[:4], rest[4:]
    x, w_mine, zl_mine, y_mine = (lax.axis_index(name) for name in ("x", "w", "zl", "y"))
    total = jnp.sum(in_ref[...].astype(F32).reshape(16, 4, 8, 256), axis=1).reshape(128, 256)
    first_mode = (x == 0) & (w_mine == 0) & (zl_mine == 0)
    is_u = (lax.broadcasted_iota(jnp.int32, (128, 256), 0) & 2) != 0
    g_scale = jnp.where(first_mode, factor, 2.0 * factor)
    low = (total * jnp.where(is_u, factor, g_scale)).astype(BF16)
    digits = [(32, 2, 2), (8, 4, 8), (4, 2, 1), (1, 4, 32)]
    row = lax.broadcasted_iota(jnp.int32, (32, 128), 0)
    col = lax.broadcasted_iota(jnp.int32, (32, 128), 1)
    source = ((row >> 3) << 3) + (((row >> 2) & 1) ^ 1) + ((row & 3) << 5)
    sign = jnp.where((row & 4) == 0, 1.0, -1.0)
    both = []
    for h in range(2):
        turns = jnp.where(source + 4 * h == col, sign, 0.0).astype(BF16)
        moves = row_moves((64, 128), digits, base=4 * h)
        both.append(dot(jnp.concatenate([moves, turns], axis=0), low))
    both = jnp.concatenate(both, axis=1)
    g, u = both[:32], both[32:64]
    g_low, g_turned = g.astype(BF16), both[64:].astype(BF16)
    grad = (dot(g_low, w_ref[0], NT) + dot(g_turned, w_ref[1], NT)).astype(BF16)
    out = None
    for q in range(4):
        moves = row_moves((128, 32), [(32, 4, 1), (8, 4, 8), (1, 2, 4)], [(2, 4, q)])
        part = dot(moves, grad[:, 128 * q : 128 * q + 128])
        out = part if out is None else out + part
    out = out.reshape(16, 8, 128).astype(BF16)
    for zl in range(4):
        out_ref[:, zl] = out
    copy = pltpu.make_async_copy(out_ref, out_hbm, sem)
    copy.start()
    for y in range(4):
        lanes = slice(128 * y, 128 * y + 128)
        chunks[y] = jnp.concatenate([g[8 * w : 8 * w + 8, lanes] for w in range(4)], axis=1)
    for t in range(4):
        chunk = chunks[(y_mine + t) & 3]
        side_refs[t][...] = jnp.concatenate([u, chunk], axis=0).astype(BF16)
    copy.wait()


def weight_kernel(*refs):
    in_refs, own_ref, send_refs, result = refs[:4], refs[4], refs[5:8], refs[8]
    u = jnp.concatenate([ref[0:32, :] for ref in in_refs], axis=0)
    g = jnp.concatenate(
        [ref[32:40, 128 * w : 128 * w + 128].astype(F32) for ref in in_refs for w in range(4)],
        axis=0,
    ).astype(BF16)
    both = jnp.concatenate([g, dot(turned(128), g).astype(BF16)], axis=1)
    result[...] = dot(both, u, TN).reshape(2, 4, 32, 512)
    zl_mine = lax.axis_index("zl")
    own_ref[...] = result[:, zl_mine]
    for t in range(1, 4):
        send_refs[t - 1][...] = result[:, (zl_mine + t) & 3].reshape(64, 512).astype(BF16)


def transform(factor, step, in_ref, table_ref, rows, out, field_hbm, sem):
    rows[...] = in_ref[...].astype(F32).reshape(512, 128)
    b = (lax.axis_index("y") - step) & 3
    copies = []
    for h in range(2):
        modes = [
            jnp.concatenate([rows[pl.ds(2 * q + p, 64, stride=8), :] for p in range(2)], axis=0)
            for q in (2 * h, 2 * h + 1)
        ]
        modes = jnp.concatenate(modes, axis=1).astype(BF16)
        out[h] = (dot(table_ref[...], modes) * factor).astype(BF16)
        lanes = slice(256 * h, 256 * h + 256)
        copies.append(pltpu.make_async_copy(out.at[h], field_hbm.at[b, :, lanes], sem.at[h]))
        copies[-1].start()
    return copies


def own_field_kernel(factor, in_ref, field_hbm, table_ref, rows, out, sem):
    points = table_ref.shape[0]
    offset = (lax.axis_index("y") * 4 + lax.axis_index("zl")) * points
    table_ref[...] = table_of(points, True, offset)
    for copy in transform(factor, 0, in_ref, table_ref, rows, out, field_hbm, sem):
        copy.wait()


def last_kernel(factor, *refs):
    in_refs, table_ref, own_ref, weight_in = refs[:3], refs[3], refs[4], refs[5:8]
    field_hbm, weight_hbm, rows, out, weights, sem, weight_sem = refs[9:]
    zl_mine = lax.axis_index("zl")
    copies = [pltpu.make_async_copy(own_ref, weight_hbm.at[zl_mine], weight_sem.at[0])]
    copies[0].start()
    for t in range(1, 4):
        weights[t - 1] = weight_in[t - 1][...].astype(F32).reshape(2, 32, 512)
        target = weight_hbm.at[(zl_mine - t) & 3]
        copies.append(pltpu.make_async_copy(weights.at[t - 1], target, weight_sem.at[t]))
        copies[-1].start()
    for i, t in enumerate((1, 3, 2)):
        copies += transform(factor, t, in_refs[i], table_ref, rows.at[i], out.at[i], field_hbm, sem.at[i])
    for copy in copies:
        copy.wait()


def shifted(value, axis, distance):
    return lax.ppermute(value, axis, [(i, (i + distance) % 4) for i in range(4)])


def cost(flops, bytes_accessed):
    return pl.CostEstimate(flops=flops, bytes_accessed=bytes_accessed, transcendentals=0)


def shards(fields, pre_act, cotangent, weights):
    total = fields.shape[1] * lax.axis_size("y") * lax.axis_size("zl")
    factor = float(total) ** (-0.5)
    vmem = pl.BlockSpec(memory_space=pltpu.VMEM)
    hbm = pl.BlockSpec(memory_space=pltpu.HBM)
    params = pltpu.CompilerParams(vmem_limit_bytes=40 * 2**20)

    def block(*shape):
        return jax.ShapeDtypeStruct(shape, BF16)

    def spectra(steps, after):
        n = len(steps)
        moves = [block(2, 512, 256)] if steps == (0,) else []
        return pl.pallas_call(
            functools.partial(spectra_kernel, steps),
            in_specs=[hbm] * 4,
            out_specs=[vmem] + [hbm] * n + [vmem] * len(moves),
            out_shape=[jax.ShapeDtypeStruct((8, 128), F32)] + [block(256, 512)] * n + moves,
            scratch_shapes=[pltpu.VMEM((256, 512), BF16)] * n
            + [pltpu.VMEM((n, 512, 512), BF16)] * 3
            + [pltpu.VMEM((128, 512), BF16), pltpu.SemaphoreType.DMA((3, n, 2))]
            + [pltpu.SemaphoreType.DMA((n, 2))],
            compiler_params=pltpu.CompilerParams(vmem_limit_bytes=52 * 2**20),
            cost_estimate=cost(2**28 * n, 2**22 * n),
            name="spectra",
        )(fields, pre_act, cotangent, after)

    token, two = spectra((2,), fields)
    token, one, three = spectra((1, 3), token)
    _, own, moves = spectra((0,), token)
    one, two, three = shifted(one, "y", 1), shifted(two, "y", 2), shifted(three, "y", 3)
    send = pl.pallas_call(
        sum_y_kernel,
        in_specs=[vmem] * 5,
        out_specs=hbm,
        out_shape=block(64, 8, 256),
        scratch_shapes=[pltpu.VMEM((64, 8, 256), BF16), pltpu.SemaphoreType.DMA((2,))],
        compiler_params=params,
        name="sum_y",
    )(moves, own, one, two, three)
    got = lax.all_to_all(send, OTHERS, 0, 0, tiled=True)
    mine = lax.dynamic_index_in_dim(weights, lax.axis_index("zl"), 0, keepdims=False)
    send, *sides = pl.pallas_call(
        functools.partial(modes_kernel, factor),
        in_specs=[vmem, vmem],
        out_specs=[hbm] + [vmem] * 4,
        out_shape=[block(16, 4, 8, 128)] + [block(40, 512)] * 4,
        scratch_shapes=[
            pltpu.VMEM((4, 8, 512), F32),
            pltpu.VMEM((16, 4, 8, 128), BF16),
            pltpu.SemaphoreType.DMA,
        ],
        compiler_params=params,
        name="modes",
    )(got, mine)
    sides = [sides[0]] + [shifted(sides[t], "y", t) for t in range(1, 4)]
    got = lax.all_to_all(send.reshape(64, 8, 128), OTHERS, 0, 0, tiled=True)
    own_weight, *sides = pl.pallas_call(
        weight_kernel,
        in_specs=[vmem] * 4,
        out_specs=[vmem] * 4,
        out_shape=[jax.ShapeDtypeStruct((2, 32, 512), F32)] + [block(64, 512)] * 3,
        scratch_shapes=[pltpu.VMEM((2, 4, 32, 512), F32)],
        compiler_params=params,
        cost_estimate=cost(2**26, 2**20),
        name="weight",
    )(*sides)
    sides = [shifted(sides[t - 1], "zl", t) for t in range(1, 4)]
    received = [shifted(got, "y", t) for t in (1, 3, 2)]
    field_grad, table = pl.pallas_call(
        functools.partial(own_field_kernel, factor),
        in_specs=[vmem],
        out_specs=[hbm, vmem],
        out_shape=[block(4, 512, 512), block(512, 128)],
        scratch_shapes=[
            pltpu.VMEM((512, 128), F32),
            pltpu.VMEM((2, 512, 256), BF16),
            pltpu.SemaphoreType.DMA((2,)),
        ],
        compiler_params=params,
        cost_estimate=cost(2**27, 2**20),
        name="own_field",
    )(got)
    field_grad, weight_grad = pl.pallas_call(
        functools.partial(last_kernel, factor),
        in_specs=[vmem] * 8 + [hbm],
        out_specs=[hbm, hbm],
        out_shape=[block(4, 512, 512), jax.ShapeDtypeStruct((4, 2, 32, 512), F32)],
        scratch_shapes=[
            pltpu.VMEM((3, 512, 128), F32),
            pltpu.VMEM((3, 2, 512, 256), BF16),
            pltpu.VMEM((3, 2, 32, 512), F32),
            pltpu.SemaphoreType.DMA((3, 2)),
            pltpu.SemaphoreType.DMA((4,)),
        ],
        input_output_aliases={8: 0},
        compiler_params=params,
        name="last",
    )(*received, table, own_weight, *sides, field_grad)
    return field_grad, jnp.swapaxes(weight_grad, 2, 3)


def solution(mesh):
    grid = Mesh(mesh.devices.reshape(4, 4, 4, 4), ("y", "zl", "x", "w"))
    space, mode = ("y", "zl"), ("x", "w")
    whole = P(mode, space, None)
    return jax.shard_map(
        shards,
        mesh=grid,
        in_specs=(whole, whole, whole, P(mode, None, None, None)),
        out_specs=(whole, P(mode, None, None, space)),
        check_vma=False,
    )
```
